512 devices in a mesh: fsdp: 64 (over x, z, core), tensor: 8 (over y).
Axes of the slice: x: 4, y: 8, z: 8, core: 2. Of those that a mesh axis runs over, the one named last changes fastest.
Arguments:
- grads: bfloat16 [64, 1024, 1024], P('fsdp', 'tensor'), may hold values from -6 to 6
- row_counts: int32 [64], replicated, may hold values from 512 to 1024, as said below
- col_counts: int32 [64], replicated, may hold values from 512 to 1024, as said below
- old_left: bfloat16 [64, 1024, 1024], P('fsdp', 'tensor'), may hold values from -1 to 2
- old_right: bfloat16 [64, 1024, 1024], P('fsdp', 'tensor'), may hold values from -1 to 2
Outputs:
- new_left: bfloat16 [64, 1024, 1024], P('fsdp', 'tensor')
- new_right: bfloat16 [64, 1024, 1024], P('fsdp', 'tensor')
The draws below stay inside these ranges and needn't reach their ends.
Inputs may be any that keep to these rules, and one draw needn't show every extreme that they name: `row_counts`: a multiple of 128; some block has all 1024 rows. `col_counts`: a multiple of 128; some block has all 1024 columns.
All inputs are finite; a program needn't handle non-finite values.
Results may differ from the reference program's by a relative error of at most 0.0068.
Values may be sent and summed in bfloat16 or wider, within the bound.
A program may use at most 128 MiB of HBM per device.

```python
import math
import jax
import jax.numpy as jnp
from jax import lax

BLOCK = 1024
NBLK = 64


def counts_from(key):
    first, second = jax.random.split(key)
    base = BLOCK // 8 * jax.random.randint(first, (NBLK,), 4, 9)
    place = jax.random.randint(second, (), 0, NBLK)
    return base.at[place].set(BLOCK).astype(jnp.int32)


def basis_from(key):
    noise = jnp.clip(jax.random.normal(key, (NBLK, BLOCK, BLOCK), jnp.float32), -6.0, 6.0)
    values = jnp.eye(BLOCK, dtype=jnp.float32)[None] + 0.25 / math.sqrt(BLOCK) * noise
    return values.astype(jnp.bfloat16)


def draw_row_counts(key, part):
    key = jax.random.fold_in(key, 11)
    return counts_from(key)


def draw_col_counts(key, part):
    key = jax.random.fold_in(key, 23)
    return counts_from(key)


def draw_old_left(key, part):
    key = jax.random.fold_in(key, 37)
    return basis_from(key)


def draw_old_right(key, part):
    key = jax.random.fold_in(key, 41)
    return basis_from(key)


def block_levels(own_key, shape, cuts, low, high):
    loudness = 1.0
    for axis_at, blocks in cuts:
        steps = jax.random.uniform(jax.random.fold_in(jax.random.fold_in(own_key, 6), axis_at), (blocks,), jnp.float32, low / len(cuts), high / len(cuts))
        loudness = loudness * jnp.repeat(jnp.exp(steps), shape[axis_at] // blocks).reshape((-1,) + (1,) * (len(shape) - 1 - axis_at))
    return loudness


def centred(rng, dims, scale, limit, shards=(), held_as=jnp.bfloat16):
    loudness = block_levels(rng, dims, shards, -0.22, 0.18) if shards else 1.0
    values = jax.random.normal(rng, dims, jnp.float32) * scale * loudness
    return jnp.minimum(jnp.maximum(values, -limit), limit).astype(held_as)


def setup_inputs(seed: int = 0) -> dict:
    key_list = jax.random.split(jax.random.key(seed), 6)
    return {
        "grads": centred(key_list[0], (NBLK, BLOCK, BLOCK), 1.0, 6.0, ((0, 64), (1, 8))),
        "row_counts": draw_row_counts(jax.random.fold_in(key_list[5], 71), 0),
        "col_counts": draw_col_counts(jax.random.fold_in(key_list[5], 71), 0),
        "old_left": draw_old_left(jax.random.fold_in(key_list[5], 71), 0),
        "old_right": draw_old_right(jax.random.fold_in(key_list[5], 71), 0),
    }


def refresh(stat, basis):
    power = (jnp.dot(stat.astype(jnp.float32), basis.astype(jnp.float32), preferred_element_type=jnp.float32) + basis.astype(jnp.float32)).astype(jnp.bfloat16)
    gram = jnp.dot(power.T.astype(jnp.float32), power.astype(jnp.float32), preferred_element_type=jnp.float32)
    lower = jnp.linalg.cholesky(gram)
    solved = jax.scipy.linalg.solve_triangular(lower, power.astype(jnp.float32).T, lower=True)
    return solved.T.astype(jnp.bfloat16)

def one_block(items):
    grad, rows_valid, cols_valid, left_basis, right_basis = items
    row_ids = jnp.arange(BLOCK, dtype=jnp.int32)
    keep = (row_ids[:, None] < rows_valid) & (row_ids[None, :] < cols_valid)
    kept = jnp.where(keep, grad, jnp.zeros_like(grad)).astype(jnp.bfloat16)
    left_stat = (jnp.dot(kept.astype(jnp.float32), kept.T.astype(jnp.float32), preferred_element_type=jnp.float32) / BLOCK).astype(jnp.bfloat16)
    right_stat = (jnp.dot(kept.T.astype(jnp.float32), kept.astype(jnp.float32), preferred_element_type=jnp.float32) / BLOCK).astype(jnp.bfloat16)
    return (refresh(left_stat, left_basis), refresh(right_stat, right_basis))

def reference(grads, row_counts, col_counts, old_left, old_right):
    new_left, new_right = lax.map(one_block, (grads, row_counts, col_counts, old_left, old_right))
    return (new_left, new_right)
```

```python
import functools

import jax
import jax.numpy as jnp
from jax import lax
from jax.experimental import pallas as pl
from jax.experimental.pallas import tpu as pltpu
from jax.sharding import PartitionSpec as P

MESH = pl.DeviceIdType.MESH
BF16 = jnp.bfloat16
F32 = jnp.float32
NB = 128
VMEM_LIMIT = 56 * 1024 * 1024


def workers(lanes):
    core = lax.rem(lax.axis_index("fsdp"), 2)
    left = core * (lanes // 4)
    return left, left + lanes // 2


def ring_barrier(lanes, me):
    barrier = pltpu.get_barrier_semaphore()
    for step in range(1, lanes):
        other = lax.rem(me + step, lanes)
        pl.semaphore_signal(barrier, inc=1, device_id={"tensor": other}, device_id_type=MESH)
    pl.semaphore_wait(barrier, lanes - 1)


def gather_kernel(lanes, rc_ref, cc_ref, g_ref, l_ref, r_ref, gout, pout, gm, ssem, gsem, psem, osem):
    me = lax.axis_index("tensor")
    block = lax.axis_index("fsdp")
    rows, side = g_ref.shape
    left, right = workers(lanes)
    rid = me * rows + lax.broadcasted_iota(jnp.int32, (rows, side), 0)
    cid = lax.broadcasted_iota(jnp.int32, (rows, side), 1)
    keep = (rid < rc_ref[block]) & (cid < cc_ref[block])
    gm[...] = jnp.where(keep, g_ref[...].astype(F32), 0.0).astype(BF16)
    ring_barrier(lanes, me)
    mine = pl.ds(pl.multiple_of(me * rows, rows), rows)

    def remote(src, dst, k, sem, to):
        return pltpu.make_async_remote_copy(
            src_ref=src, dst_ref=dst.at[mine], send_sem=ssem.at[k], recv_sem=sem.at[me],
            device_id={"tensor": to}, device_id_type=MESH,
        )

    jobs = []
    for k, (src, dst, sem, to) in enumerate(
        ((gm, gout, gsem, left), (gm, gout, gsem, right), (l_ref, pout, psem, left), (r_ref, pout, psem, right))
    ):
        jobs.append((to, src, dst, k, remote(src, dst, k, sem, to)))
    for to, src, dst, k, copy in jobs:
        @pl.when(me != to)
        def _():
            copy.start()

        @pl.when(me == to)
        def _():
            pltpu.make_async_copy(src, dst.at[mine], osem.at[k]).start()
    for to, src, dst, k, copy in jobs:
        @pl.when(me != to)
        def _():
            copy.wait_send()

        @pl.when(me == to)
        def _():
            pltpu.make_async_copy(src, dst.at[mine], osem.at[k]).wait()

    @pl.when((me == left) | (me == right))
    def _():
        for step in range(1, lanes):
            other = lax.rem(me + step, lanes)
            theirs = pl.ds(pl.multiple_of(other * rows, rows), rows)
            for src, dst, sem in ((gm, gout, gsem), (l_ref, pout, psem)):
                pltpu.make_async_remote_copy(
                    src_ref=src, dst_ref=dst.at[theirs], send_sem=ssem.at[0], recv_sem=sem.at[other],
                    device_id={"tensor": other}, device_id_type=MESH,
                ).wait_recv()


def scatter_kernel(lanes, x_ref, lout, rout, ssem, rsem, osem):
    me = lax.axis_index("tensor")
    rows = lout.shape[0]
    left, right = workers(lanes)
    ring_barrier(lanes, me)

    def copy_to(which, out, step):
        other = lax.rem(me + step, lanes)
        theirs = pl.ds(pl.multiple_of(other * rows, rows), rows)
        return pltpu.make_async_remote_copy(
            src_ref=x_ref.at[theirs], dst_ref=out, send_sem=ssem.at[step], recv_sem=rsem.at[which],
            device_id={"tensor": other}, device_id_type=MESH,
        )

    mine = pl.ds(pl.multiple_of(me * rows, rows), rows)
    for which, (worker, out) in enumerate(((left, lout), (right, rout))):
        @pl.when(me == worker)
        def _():
            for step in range(1, lanes):
                copy_to(which, out, step).start()
            pltpu.make_async_copy(x_ref.at[mine], out, osem).start()
            for step in range(1, lanes):
                copy_to(which, out, step).wait_send()
            pltpu.make_async_copy(x_ref.at[mine], out, osem).wait()

    for which, (worker, out) in enumerate(((left, lout), (right, rout))):
        @pl.when(me != worker)
        def _():
            copy_to(which, out, 1).wait_recv()


def across(column):
    return jnp.broadcast_to(column, (8, NB))


def inverse_rcp(x):
    r = pl.reciprocal(x, approx=True)
    return r * (2.0 - x * r)


def diag_inverse(load):
    count = NB // 8
    sub = lax.broadcasted_iota(jnp.int32, (8, NB), 0)
    lane = lax.broadcasted_iota(jnp.int32, (8, NB), 1)
    rows = [load(i) for i in range(count)]
    done = []
    for r in range(count):
        k0 = 8 * r
        inside = (lane >= k0) & (lane < k0 + 8)
        top = rows[r]
        cols = [across(top[:, k0 + q : k0 + q + 1]) for q in range(8)]
        top = jnp.where(lane - k0 == sub, 1.0, jnp.where(inside, 0.0, top))
        rcp, upper, flat = [], [], []
        scale = jnp.zeros((8, NB), F32)
        for p in range(8):
            pivot = across(cols[p][p : p + 1, :])
            inv = inverse_rcp(pivot)
            scale = jnp.where(sub == p, lax.rsqrt(pivot), scale)
            mult = jnp.where(sub > p, cols[p] * inv, 0.0)
            line = {}
            for q in range(p + 1, 8):
                line[q] = across(cols[q][p : p + 1, :])
                cols[q] = cols[q] - mult * line[q]
            row = across(top[p : p + 1, :])
            top = top - mult * row
            rcp.append(inv)
            upper.append(line)
            flat.append(row)
        done.append(jnp.where(lane <= sub + k0, top * scale, 0.0))
        for i in range(r + 1, count):
            body = rows[i]
            cols = [across(body[:, k0 + q : k0 + q + 1]) for q in range(8)]
            body = jnp.where(inside, 0.0, body)
            for p in range(8):
                w = cols[p] * rcp[p]
                for q in range(p + 1, 8):
                    cols[q] = cols[q] - w * upper[p][q]
                body = body - w * flat[p]
            rows[i] = body
    return done


def halves(x):
    high = x.astype(BF16)
    return high, (x - high.astype(F32)).astype(BF16)


def nt(a, b):
    return lax.dot_general(a, b, (((1,), (1,)), ((), ())), preferred_element_type=F32)


def nn(a, b):
    return jnp.dot(a, b, preferred_element_type=F32)


def tn(a, b):
    return lax.dot_general(a, b, (((0,), (0,)), ((), ())), preferred_element_type=F32)


def refresh_kernel(role_ref, g_ref, p_ref, x_ref, s_ref, w_ref, a_ref, nh, nl, lcat, rcat, m_ref):
    side = g_ref.shape[0]
    tile = min(256, side)
    tiles = side // tile
    role = role_ref[0]

    def at(t):
        return pl.ds(pl.multiple_of(t * tile, tile), tile)

    @pl.when(role == 0)
    def _():
        @pl.loop(0, tiles)
        def _(t):
            s_ref[at(t), :] = (nt(g_ref[at(t), :], g_ref[...]) * (1.0 / side)).astype(BF16)

    @pl.when(role == 1)
    def _():
        @pl.loop(0, tiles)
        def _(t):
            s_ref[at(t), :] = (tn(g_ref[:, at(t)], g_ref[...]) * (1.0 / side)).astype(BF16)

    @pl.when(role < 2)
    def _():
        @pl.loop(0, tiles)
        def _(t):
            w_ref[at(t), :] = (nn(s_ref[at(t), :], p_ref[...]) + p_ref[at(t), :].astype(F32)).astype(BF16)

        @pl.loop(0, tiles)
        def _(t):
            a_ref[at(t), :] = tn(w_ref[:, at(t)], w_ref[...])

        @pl.loop(0, side // NB)
        def _(j):
            start = pl.multiple_of(j * NB, NB)
            here = pl.ds(start, NB)
            done = diag_inverse(lambda i: a_ref[pl.ds(start + 8 * i, 8), here])
            for i, part in enumerate(done):
                m_ref[8 * i : 8 * i + 8, :] = part
            inv = m_ref[...]
            mh, ml = halves(inv)
            rid = lax.broadcasted_iota(jnp.int32, (side, NB), 0)
            column = a_ref[:, here]
            below = rid >= start + NB
            ch, cl = halves(jnp.where(below, column, 0.0))
            low = nt(ch, mh) + nt(cl, mh) + nt(ch, ml)
            lh, ll = halves(low)
            lcat[:, 0:NB] = lh
            lcat[:, NB : 2 * NB] = ll
            lcat[:, 2 * NB : 3 * NB] = lh
            a_ref[:, here] = jnp.where(below, 0.0, column)
            bh, bl = halves(a_ref[here, :])
            rcat[0:NB, :] = bh
            rcat[NB : 2 * NB, :] = bh
            rcat[2 * NB : 3 * NB, :] = bl
            fresh = nn(jnp.concatenate([mh, ml, mh], axis=1), rcat[...])
            a_ref[here, :] = fresh
            a_ref[here, here] = inv
            fh, fl = halves(a_ref[here, :])
            rcat[0:NB, :] = fh
            rcat[NB : 2 * NB, :] = fh
            rcat[2 * NB : 3 * NB, :] = fl
            cid = lax.broadcasted_iota(jnp.int32, (NB, side), 1)
            kept = cid < start + NB
            nh[here, :] = jnp.where(kept, fh.astype(F32), 0.0).astype(BF16)
            nl[here, :] = jnp.where(kept, fl.astype(F32), 0.0).astype(BF16)

            @pl.loop((j + 1) * NB // tile, tiles)
            def _(t):
                a_ref[at(t), :] = a_ref[at(t), :] - nn(lcat[at(t), :], rcat[...])

        @pl.loop(0, tiles)
        def _(t):
            x_ref[at(t), :] = (nt(w_ref[at(t), :], nh[...]) + nt(w_ref[at(t), :], nl[...])).astype(BF16)


def refresh_call(role, grad, basis):
    side = grad.shape[0]
    vmem = pl.BlockSpec(memory_space=pltpu.VMEM)
    return pl.pallas_call(
        refresh_kernel,
        out_shape=jax.ShapeDtypeStruct((side, side), BF16),
        in_specs=[pl.BlockSpec(memory_space=pltpu.SMEM), vmem, vmem],
        out_specs=vmem,
        scratch_shapes=[
            pltpu.VMEM((side, side), BF16),
            pltpu.VMEM((side, side), BF16),
            pltpu.VMEM((side, side), F32),
            pltpu.VMEM((side, side), BF16),
            pltpu.VMEM((side, side), BF16),
            pltpu.VMEM((side, 3 * NB), BF16),
            pltpu.VMEM((3 * NB, side), BF16),
            pltpu.VMEM((NB, NB), F32),
        ],
        compiler_params=pltpu.CompilerParams(vmem_limit_bytes=VMEM_LIMIT),
        cost_estimate=pl.CostEstimate(flops=14 * side**3, bytes_accessed=6 * side * side, transcendentals=0),
        name="refresh",
    )(role, grad, basis)


def body(grads, row_counts, col_counts, old_left, old_right):
    rows, side = grads.shape[1:]
    lanes = lax.axis_size("tensor")
    me = lax.axis_index("tensor")
    vmem = pl.BlockSpec(memory_space=pltpu.VMEM)
    smem = pl.BlockSpec(memory_space=pltpu.SMEM)
    hbm = pl.BlockSpec(memory_space=pl.ANY)
    whole = jax.ShapeDtypeStruct((side, side), BF16)
    part = jax.ShapeDtypeStruct((rows, side), BF16)
    dma = pltpu.SemaphoreType.DMA
    grad, basis = pl.pallas_call(
        functools.partial(gather_kernel, lanes),
        out_shape=(whole, whole),
        in_specs=[smem, smem, vmem, vmem, vmem],
        out_specs=(hbm, hbm),
        scratch_shapes=[pltpu.VMEM((rows, side), BF16), dma((4,)), dma((lanes,)), dma((lanes,)), dma((4,))],
        compiler_params=pltpu.CompilerParams(
            collective_id=0, has_side_effects=True, vmem_limit_bytes=VMEM_LIMIT
        ),
        name="gather",
    )(row_counts, col_counts, grads[0], old_left[0], old_right[0])
    left, right = workers(lanes)
    role = jnp.where(me == left, 0, jnp.where(me == right, 1, 2)).astype(jnp.int32).reshape(1)
    fresh = refresh_call(role, grad, basis)
    new_left, new_right = pl.pallas_call(
        functools.partial(scatter_kernel, lanes),
        out_shape=(part, part),
        in_specs=[hbm],
        out_specs=(hbm, hbm),
        scratch_shapes=[dma((lanes,)), dma((2,)), dma],
        compiler_params=pltpu.CompilerParams(
            collective_id=1, has_side_effects=True, vmem_limit_bytes=VMEM_LIMIT
        ),
        name="scatter",
    )(fresh)
    return (new_left[None], new_right[None])


def solution(mesh):
    split = P("fsdp", "tensor", None)
    return jax.shard_map(
        body, mesh=mesh, in_specs=(split, P(), P(), split, split), out_specs=(split, split), check_vma=False
    )
```

```python
import functools

import jax
import jax.numpy as jnp
from jax import lax
from jax.experimental import pallas as pl
from jax.experimental.pallas import tpu as pltpu
from jax.sharding import PartitionSpec as P

MESH = pl.DeviceIdType.MESH
BF16 = jnp.bfloat16
F32 = jnp.float32
NB = 128
VMEM_LIMIT = 56 * 1024 * 1024


def workers(lanes):
    core = lax.rem(lax.axis_index("fsdp"), 2)
    left = core * (lanes // 4)
    return left, left + lanes // 2


def ring_barrier(lanes, me):
    barrier = pltpu.get_barrier_semaphore()
    for step in range(1, lanes):
        other = lax.rem(me + step, lanes)
        pl.semaphore_signal(barrier, inc=1, device_id={"tensor": other}, device_id_type=MESH)
    pl.semaphore_wait(barrier, lanes - 1)


def across(column):
    return jnp.broadcast_to(column, (8, NB))


def inverse_rcp(x):
    r = pl.reciprocal(x, approx=True)
    return r * (2.0 - x * r)


def diag_inverse(load):
    count = NB // 8
    sub = lax.broadcasted_iota(jnp.int32, (8, NB), 0)
    lane = lax.broadcasted_iota(jnp.int32, (8, NB), 1)
    rows = [load(i) for i in range(count)]
    done = []
    for r in range(count):
        k0 = 8 * r
        inside = (lane >= k0) & (lane < k0 + 8)
        top = rows[r]
        cols = [across(top[:, k0 + q : k0 + q + 1]) for q in range(8)]
        top = jnp.where(lane - k0 == sub, 1.0, jnp.where(inside, 0.0, top))
        rcp, upper, flat = [], [], []
        scale = jnp.zeros((8, NB), F32)
        for p in range(8):
            pivot = across(cols[p][p : p + 1, :])
            inv = inverse_rcp(pivot)
            scale = jnp.where(sub == p, lax.rsqrt(pivot), scale)
            mult = jnp.where(sub > p, cols[p] * inv, 0.0)
            line = {}
            for q in range(p + 1, 8):
                line[q] = across(cols[q][p : p + 1, :])
                cols[q] = cols[q] - mult * line[q]
            row = across(top[p : p + 1, :])
            top = top - mult * row
            rcp.append(inv)
            upper.append(line)
            flat.append(row)
        done.append(jnp.where(lane <= sub + k0, top * scale, 0.0))
        for i in range(r + 1, count):
            body = rows[i]
            cols = [across(body[:, k0 + q : k0 + q + 1]) for q in range(8)]
            body = jnp.where(inside, 0.0, body)
            for p in range(8):
                w = cols[p] * rcp[p]
                for q in range(p + 1, 8):
                    cols[q] = cols[q] - w * upper[p][q]
                body = body - w * flat[p]
            rows[i] = body
    return done


def halves(x):
    high = x.astype(BF16)
    return high, (x - high.astype(F32)).astype(BF16)


def nt(a, b):
    return lax.dot_general(a, b, (((1,), (1,)), ((), ())), preferred_element_type=F32)


def nn(a, b):
    return jnp.dot(a, b, preferred_element_type=F32)


def tn(a, b):
    return lax.dot_general(a, b, (((0,), (0,)), ((), ())), preferred_element_type=F32)


def eliminate(step, a_ref, m_ref, lcat, rcat, pair):
    side = a_ref.shape[0]
    start = pl.multiple_of(step * NB, NB)
    here = pl.ds(start, NB)
    mh, ml = halves(m_ref[...])
    scale_row(step, a_ref, m_ref, mh, ml, rcat, pair)
    below = lax.broadcasted_iota(jnp.int32, (side, NB), 0) >= start + NB
    column = a_ref[:, here]
    ch, cl = halves(jnp.where(below, column, 0.0))
    low = nt(jnp.concatenate([ch, cl, ch], axis=1), jnp.concatenate([mh, mh, ml], axis=1))
    lh, ll = halves(low)
    lcat[:, 0:NB] = lh
    lcat[:, NB : 2 * NB] = ll
    lcat[:, 2 * NB : 3 * NB] = lh
    a_ref[:, here] = jnp.where(below, 0.0, column)
    tile = min(256, side)
    for t in range(side // tile):
        cols = slice(t * tile, (t + 1) * tile)
        a_ref[:, cols] = a_ref[:, cols] - nn(lcat[...], rcat[:, cols])


def scale_row(step, a_ref, m_ref, mh, ml, rcat, pair):
    side = a_ref.shape[0]
    start = pl.multiple_of(step * NB, NB)
    here = pl.ds(start, NB)
    bh, bl = halves(a_ref[here, :])
    fresh = nn(
        jnp.concatenate([mh, ml, mh], axis=1), jnp.concatenate([bh, bh, bl], axis=0)
    )
    a_ref[here, :] = fresh
    a_ref[here, here] = m_ref[...]
    fresh = a_ref[here, :]
    fh, fl = halves(fresh)
    rcat[0:NB, :] = fh
    rcat[NB : 2 * NB, :] = fh
    rcat[2 * NB : 3 * NB, :] = fl
    kept = lax.broadcasted_iota(jnp.int32, (NB, side), 1) < start + NB
    kh, kl = halves(jnp.where(kept, fresh, 0.0))
    pair[0:NB, :] = kh
    pair[NB : 2 * NB, :] = kl


def kernel(
    lanes, rc_ref, cc_ref, g_in, l_in, r_in, out,
    gm, gbuf, pbuf, s_ref, w_ref, x_ref, a_ref, lcat, rcat, pair, m_ref, d_ref,
    ssem, gsem, psem, osem, xsend, xrecv, xown,
):
    me = lax.axis_index("tensor")
    block = lax.axis_index("fsdp")
    rows, side = g_in.shape
    steps = side // NB
    tile = min(256, side)
    left, right = workers(lanes)
    ring_barrier(lanes, me)

    def rows_of(lane):
        return pl.ds(pl.multiple_of(lane * rows, rows), rows)

    mine = rows_of(me)
    rid = me * rows + lax.broadcasted_iota(jnp.int32, (rows, side), 0)
    cid = lax.broadcasted_iota(jnp.int32, (rows, side), 1)
    keep = (rid < rc_ref[block]) & (cid < cc_ref[block])
    gm[...] = jnp.where(keep, g_in[...].astype(F32), 0.0).astype(BF16)

    def remote(src, dst, k, sem, to):
        return pltpu.make_async_remote_copy(
            src_ref=src, dst_ref=dst.at[mine], send_sem=ssem.at[k], recv_sem=sem.at[me],
            device_id={"tensor": to}, device_id_type=MESH,
        )

    jobs = (
        (left, gm, gbuf, 0, gsem), (right, gm, gbuf, 1, gsem), (left, l_in, pbuf, 2, psem), (right, r_in, pbuf, 3, psem)
    )
    for to, src, dst, k, sem in jobs:
        @pl.when(me != to)
        def _():
            remote(src, dst, k, sem, to).start()

        @pl.when(me == to)
        def _():
            pltpu.make_async_copy(src, dst.at[mine], osem.at[k]).start()

    def finish_jobs(chosen):
        for to, src, dst, k, sem in chosen:
            @pl.when(me != to)
            def _():
                remote(src, dst, k, sem, to).wait_send()

            @pl.when(me == to)
            def _():
                pltpu.make_async_copy(src, dst.at[mine], osem.at[k]).wait()

    def arrived(src, dst, sem):
        for step in range(1, lanes):
            other = lax.rem(me + step, lanes)
            pltpu.make_async_remote_copy(
                src_ref=src, dst_ref=dst.at[rows_of(other)], send_sem=ssem.at[0], recv_sem=sem.at[other],
                device_id={"tensor": other}, device_id_type=MESH,
            ).wait_recv()

    def columns(step):
        return pl.ds(pl.multiple_of(step * NB, NB), NB)

    def give(which, step, turn):
        other = lax.rem(me + turn, lanes)
        return pltpu.make_async_remote_copy(
            src_ref=x_ref.at[rows_of(other), columns(step)], dst_ref=out.at[which, :, columns(step)],
            send_sem=xsend.at[step, turn], recv_sem=xrecv.at[which, step],
            device_id={"tensor": other}, device_id_type=MESH,
        )

    def own(which, step):
        return pltpu.make_async_copy(x_ref.at[mine, columns(step)], out.at[which, :, columns(step)], xown.at[step])

    def result(step, which):
        both = nt(w_ref[...], pair[...])
        x_ref[:, columns(step)] = (both[:, :NB] + both[:, NB:]).astype(BF16)
        for turn in range(1, lanes):
            give(which, step, turn).start()
        own(which, step).start()

    def at(t):
        return pl.ds(pl.multiple_of(t * tile, tile), tile)

    def next_diag(step):
        later = columns(lax.rem(step + 1, steps))
        mh, ml = halves(m_ref[...])
        ch, cl = halves(a_ref[later, columns(step)])
        low = nt(jnp.concatenate([ch, cl, ch], axis=1), jnp.concatenate([mh, mh, ml], axis=1))
        lh, ll = halves(low)
        d_ref[...] = a_ref[later, later] - nt(
            jnp.concatenate([lh, ll, lh], axis=1), jnp.concatenate([lh, lh, ll], axis=1)
        )

    def begin(which):
        finish_jobs(jobs[which : which + 1])
        arrived(gm, gbuf, gsem)

        @pl.loop(0, side // tile)
        def _(t):
            if which == 0:
                stat = nt(gbuf[at(t), :], gbuf[...])
            else:
                stat = tn(gbuf[:, at(t)], gbuf[...])
            s_ref[at(t), :] = (stat * (1.0 / side)).astype(BF16)

        finish_jobs(jobs[2 + which : 3 + which])
        arrived(l_in, pbuf, psem)
        finish_jobs((jobs[1 - which], jobs[3 - which]))

    for which, worker in enumerate((left, right)):
        @pl.when(me == worker)
        def _():
            begin(which)

    working = (me == left) | (me == right)
    side_of = lax.div(lax.rem(me - left + lanes, lanes), lanes // 2)

    @pl.when(working)
    def _():
        @pl.loop(0, side // tile)
        def _(t):
            w_ref[at(t), :] = (nn(s_ref[at(t), :], pbuf[...]) + pbuf[at(t), :].astype(F32)).astype(BF16)

        @pl.loop(0, side // tile)
        def _(t):
            a_ref[at(t), :] = tn(w_ref[:, at(t)], w_ref[...])

        d_ref[...] = a_ref[0:NB, 0:NB]

        def invert():
            for i, part in enumerate(diag_inverse(lambda i: d_ref[8 * i : 8 * i + 8, :])):
                m_ref[8 * i : 8 * i + 8, :] = part

        invert()
        next_diag(0)

        @pl.loop(1, steps)
        def _(step):
            eliminate(step - 1, a_ref, m_ref, lcat, rcat, pair)
            result(step - 1, side_of)
            invert()
            next_diag(step)

        mh, ml = halves(m_ref[...])
        scale_row(steps - 1, a_ref, m_ref, mh, ml, rcat, pair)
        result(steps - 1, side_of)

        @pl.loop(0, steps)
        def _(step):
            for turn in range(1, lanes):
                give(side_of, step, turn).wait_send()
            own(side_of, step).wait()

    @pl.when(jnp.logical_not(working))
    def _():
        finish_jobs(jobs)

    for which, worker in enumerate((left, right)):
        @pl.when(me != worker)
        def _():
            @pl.loop(0, steps)
            def _(step):
                give(which, step, 1).wait_recv()


def hand_on(both, c, d, sem):
    first = pltpu.make_async_copy(both.at[0], c, sem.at[0])
    second = pltpu.make_async_copy(both.at[1], d, sem.at[1])
    first.start()
    second.start()
    first.wait()
    second.wait()


def body(grads, row_counts, col_counts, old_left, old_right):
    rows, side = grads.shape[1:]
    lanes = lax.axis_size("tensor")
    steps = side // NB
    vmem = pl.BlockSpec(memory_space=pltpu.VMEM)
    smem = pl.BlockSpec(memory_space=pltpu.SMEM)
    hbm = pl.BlockSpec(memory_space=pl.ANY)
    part = jax.ShapeDtypeStruct((rows, side), BF16)
    dma = pltpu.SemaphoreType.DMA
    whole = pltpu.VMEM((side, side), BF16)
    square = pltpu.VMEM((NB, NB), F32)
    both = pl.pallas_call(
        functools.partial(kernel, lanes),
        out_shape=jax.ShapeDtypeStruct((2, rows, side), BF16),
        in_specs=[smem, smem, vmem, vmem, vmem],
        out_specs=hbm,
        scratch_shapes=[
            pltpu.VMEM((rows, side), BF16),
            whole, whole, whole, whole, whole,
            pltpu.VMEM((side, side), F32),
            pltpu.VMEM((side, 3 * NB), BF16),
            pltpu.VMEM((3 * NB, side), BF16),
            pltpu.VMEM((2 * NB, side), BF16),
            square, square,
            dma((4,)), dma((lanes,)), dma((lanes,)), dma((4,)),
            dma((steps, lanes)), dma((2, steps)), dma((steps,)),
        ],
        compiler_params=pltpu.CompilerParams(
            collective_id=0, has_side_effects=True, vmem_limit_bytes=VMEM_LIMIT
        ),
        cost_estimate=pl.CostEstimate(flops=14 * side**3, bytes_accessed=6 * side * side, transcendentals=0),
        name="refresh",
    )(row_counts, col_counts, grads[0], old_left[0], old_right[0])
    new_left, new_right = pl.pallas_call(
        hand_on,
        out_shape=(part, part),
        in_specs=[hbm],
        out_specs=(hbm, hbm),
        scratch_shapes=[dma((2,))],
        name="hand_on",
    )(both)
    return (new_left[None], new_right[None])


def solution(mesh):
    split = P("fsdp", "tensor", None)
    return jax.shard_map(
        body, mesh=mesh, in_specs=(split, P(), P(), split, split), out_specs=(split, split), check_vma=False
    )
```

```python
import functools

import jax
import jax.numpy as jnp
from jax import lax
from jax.experimental import pallas as pl
from jax.experimental.pallas import tpu as pltpu
from jax.sharding import PartitionSpec as P

MESH = pl.DeviceIdType.MESH
BF16 = jnp.bfloat16
F32 = jnp.float32
NB = 128
VMEM_LIMIT = 56 * 1024 * 1024


def workers(lanes):
    core = lax.rem(lax.axis_index("fsdp"), 2)
    left = core * (lanes // 4)
    return left, left + lanes // 2


def ring_barrier(lanes, me):
    barrier = pltpu.get_barrier_semaphore()
    for step in range(1, lanes):
        other = lax.rem(me + step, lanes)
        pl.semaphore_signal(barrier, inc=1, device_id={"tensor": other}, device_id_type=MESH)
    pl.semaphore_wait(barrier, lanes - 1)


def across(column):
    return jnp.broadcast_to(column, (8, NB))


def inverse_rcp(x):
    r = pl.reciprocal(x, approx=True)
    return r * (2.0 - x * r)


def group_update(body, inside, k0, rcp, upper, flat):
    cols = [across(body[:, k0 + q : k0 + q + 1]) for q in range(8)]
    body = jnp.where(inside, 0.0, body)
    for p in range(8):
        w = cols[p] * rcp[p]
        for q in range(p + 1, 8):
            cols[q] = cols[q] - w * upper[p][q]
        body = body - w * flat[p]
    return body


def diag_rounds(load, store):
    count = NB // 8
    sub = lax.broadcasted_iota(jnp.int32, (8, NB), 0)
    lane = lax.broadcasted_iota(jnp.int32, (8, NB), 1)
    rows = [load(i) for i in range(count)]
    for r in range(count):
        k0 = 8 * r
        inside = (lane >= k0) & (lane < k0 + 8)
        top = rows[r]
        cols = [across(top[:, k0 + q : k0 + q + 1]) for q in range(8)]
        u = [{q: across(cols[q][p : p + 1, :]) for q in range(p, 8)} for p in range(8)]
        top = jnp.where(lane - k0 == sub, 1.0, jnp.where(inside, 0.0, top))
        flat = [across(top[p : p + 1, :]) for p in range(8)]
        rcp = [None] * 8
        root = [None] * 8
        for p in range(0, 8, 2):
            n = p + 1
            det = u[p][p] * u[n][n] - u[p][n] * u[p][n]
            rcp[p] = inverse_rcp(u[p][p])
            rcp[n] = u[p][p] * inverse_rcp(det)
            root[p] = lax.rsqrt(u[p][p])
            root[n] = lax.rsqrt(det * rcp[p])
            low = {s: u[p][s] * rcp[p] for s in range(n, 8)}
            for t in range(n + 1, 8):
                u[n][t] = u[n][t] - low[n] * u[p][t]
            high = {s: u[n][s] * rcp[n] for s in range(n + 1, 8)}
            for s in range(n + 1, 8):
                for t in range(s, 8):
                    u[s][t] = u[s][t] - low[s] * u[p][t] - high[s] * u[n][t]
            flat[n] = flat[n] - low[n] * flat[p]
            for s in range(n + 1, 8):
                flat[s] = flat[s] - low[s] * flat[p] - high[s] * flat[n]
        for i in range(r + 1, min(r + 3, count)):
            rows[i] = group_update(rows[i], inside, k0, rcp, u, flat)
        scaled = jnp.zeros((8, NB), F32)
        for p in range(8):
            scaled = jnp.where(sub == p, flat[p] * root[p], scaled)
        store(r, jnp.where(lane <= sub + k0, scaled, 0.0))
        if r + 3 < count:
            high = scaled.astype(BF16).astype(F32)
            low = scaled - high
            zero = jnp.zeros((8, NB), F32)
            left = jnp.concatenate([high, low, high, zero], axis=0).astype(BF16)
            right = jnp.concatenate([high, high, low, zero], axis=0).astype(BF16)
            off = tn(left, right)
            for i in range(r + 3, count):
                rows[i] = jnp.where(inside, 0.0, rows[i]) - off[8 * i : 8 * i + 8, :]
        yield


def weave(rounds, chunks):
    chunks = list(chunks)
    total, rounds_total, given = len(chunks), NB // 8, 0
    for done, _ in enumerate(rounds, 1):
        upto = total * done // rounds_total
        for chunk in chunks[given:upto]:
            chunk()
        given = upto


def halves(x):
    high = x.astype(BF16)
    return high, (x - high.astype(F32)).astype(BF16)


def nt(a, b):
    return lax.dot_general(a, b, (((1,), (1,)), ((), ())), preferred_element_type=F32)


def nn(a, b):
    return jnp.dot(a, b, preferred_element_type=F32)


def tn(a, b):
    return lax.dot_general(a, b, (((0,), (0,)), ((), ())), preferred_element_type=F32)


def eliminate(step, a_ref, m_ref, lcat, rcat, pair):
    side = a_ref.shape[0]
    start = pl.multiple_of(step * NB, NB)
    here = pl.ds(start, NB)
    tile = min(256, side)
    spans = [slice(t * tile, (t + 1) * tile) for t in range(side // tile)]

    def scale():
        mh, ml = halves(m_ref[...])
        scale_row(step, a_ref, m_ref, mh, ml, rcat, pair)

    def multiples(span):
        mh, ml = halves(m_ref[...])
        below = span.start + lax.broadcasted_iota(jnp.int32, (tile, NB), 0) >= start + NB
        column = a_ref[span, here]
        ch, cl = halves(jnp.where(below, column, 0.0))
        low = nt(jnp.concatenate([ch, cl, ch], axis=1), jnp.concatenate([mh, mh, ml], axis=1))
        lh, ll = halves(low)
        lcat[span, 0:NB] = lh
        lcat[span, NB : 2 * NB] = ll
        lcat[span, 2 * NB : 3 * NB] = lh
        a_ref[span, here] = jnp.where(below, 0.0, column)

    def trail(rows, cols):
        a_ref[rows, cols] = a_ref[rows, cols] - nn(lcat[rows, :], rcat[:, cols])

    pieces = [scale] + [functools.partial(multiples, span) for span in spans]
    return pieces + [functools.partial(trail, rows, cols) for cols in spans for rows in spans]


def scale_row(step, a_ref, m_ref, mh, ml, rcat, pair):
    side = a_ref.shape[0]
    start = pl.multiple_of(step * NB, NB)
    here = pl.ds(start, NB)
    bh, bl = halves(a_ref[here, :])
    fresh = nn(
        jnp.concatenate([mh, ml, mh], axis=1), jnp.concatenate([bh, bh, bl], axis=0)
    )
    a_ref[here, :] = fresh
    a_ref[here, here] = m_ref[...]
    fresh = a_ref[here, :]
    fh, fl = halves(fresh)
    rcat[0:NB, :] = fh
    rcat[NB : 2 * NB, :] = fh
    rcat[2 * NB : 3 * NB, :] = fl
    kept = lax.broadcasted_iota(jnp.int32, (NB, side), 1) < start + NB
    kh, kl = halves(jnp.where(kept, fresh, 0.0))
    pair[0:NB, :] = kh
    pair[NB : 2 * NB, :] = kl


def kernel(
    lanes, rc_ref, cc_ref, g_in, l_in, r_in, out,
    gm, gbuf, pbuf, s_ref, w_ref, x_ref, a_ref, lcat, rcat, pair, m_ref, d_ref,
    ssem, gsem, psem, osem, xsend, xrecv, xown,
):
    me = lax.axis_index("tensor")
    block = lax.axis_index("fsdp")
    rows, side = g_in.shape
    steps = side // NB
    tile = min(256, side)
    left, right = workers(lanes)
    ring_barrier(lanes, me)

    def rows_of(lane):
        return pl.ds(pl.multiple_of(lane * rows, rows), rows)

    mine = rows_of(me)
    rid = me * rows + lax.broadcasted_iota(jnp.int32, (rows, side), 0)
    cid = lax.broadcasted_iota(jnp.int32, (rows, side), 1)
    keep = (rid < rc_ref[block]) & (cid < cc_ref[block])
    gm[...] = jnp.where(keep, g_in[...].astype(F32), 0.0).astype(BF16)

    def remote(src, dst, k, sem, to):
        return pltpu.make_async_remote_copy(
            src_ref=src, dst_ref=dst.at[mine], send_sem=ssem.at[k], recv_sem=sem.at[me],
            device_id={"tensor": to}, device_id_type=MESH,
        )

    jobs = (
        (left, gm, gbuf, 0, gsem), (right, gm, gbuf, 1, gsem), (left, l_in, pbuf, 2, psem), (right, r_in, pbuf, 3, psem)
    )
    for to, src, dst, k, sem in jobs:
        @pl.when(me != to)
        def _():
            remote(src, dst, k, sem, to).start()

        @pl.when(me == to)
        def _():
            pltpu.make_async_copy(src, dst.at[mine], osem.at[k]).start()

    def finish_jobs(chosen):
        for to, src, dst, k, sem in chosen:
            @pl.when(me != to)
            def _():
                remote(src, dst, k, sem, to).wait_send()

            @pl.when(me == to)
            def _():
                pltpu.make_async_copy(src, dst.at[mine], osem.at[k]).wait()

    def arrived(src, dst, sem):
        for step in range(1, lanes):
            other = lax.rem(me + step, lanes)
            pltpu.make_async_remote_copy(
                src_ref=src, dst_ref=dst.at[rows_of(other)], send_sem=ssem.at[0], recv_sem=sem.at[other],
                device_id={"tensor": other}, device_id_type=MESH,
            ).wait_recv()

    def columns(step):
        return pl.ds(pl.multiple_of(step * NB, NB), NB)

    def give(which, step, turn):
        other = lax.rem(me + turn, lanes)
        return pltpu.make_async_remote_copy(
            src_ref=x_ref.at[rows_of(other), columns(step)], dst_ref=out.at[which, :, columns(step)],
            send_sem=xsend.at[step, turn], recv_sem=xrecv.at[which, step],
            device_id={"tensor": other}, device_id_type=MESH,
        )

    def own(which, step):
        return pltpu.make_async_copy(x_ref.at[mine, columns(step)], out.at[which, :, columns(step)], xown.at[step])

    def product(step):
        def piece(t):
            span = slice(t * tile, (t + 1) * tile)
            both = nt(w_ref[span, :], pair[...])
            x_ref[span, columns(step)] = (both[:, :NB] + both[:, NB:]).astype(BF16)

        return [functools.partial(piece, t) for t in range(side // tile)]

    def send(step):
        for turn in range(1, lanes):
            give(side_of, step, turn).start()
        own(side_of, step).start()

    def at(t):
        return pl.ds(pl.multiple_of(t * tile, tile), tile)

    def next_diag(step):
        later = columns(lax.rem(step + 1, steps))
        mh, ml = halves(m_ref[...])
        ch, cl = halves(a_ref[later, columns(step)])
        low = nt(jnp.concatenate([ch, cl, ch], axis=1), jnp.concatenate([mh, mh, ml], axis=1))
        lh, ll = halves(low)
        d_ref[...] = a_ref[later, later] - nt(
            jnp.concatenate([lh, ll, lh], axis=1), jnp.concatenate([lh, lh, ll], axis=1)
        )

    def begin(which):
        finish_jobs(jobs[which : which + 1])
        arrived(gm, gbuf, gsem)

        @pl.loop(0, side // tile)
        def _(t):
            if which == 0:
                stat = nt(gbuf[at(t), :], gbuf[...])
            else:
                stat = tn(gbuf[:, at(t)], gbuf[...])
            s_ref[at(t), :] = (stat * (1.0 / side)).astype(BF16)

        finish_jobs(jobs[2 + which : 3 + which])
        arrived(l_in, pbuf, psem)
        finish_jobs((jobs[1 - which], jobs[3 - which]))

    for which, worker in enumerate((left, right)):
        @pl.when(me == worker)
        def _():
            begin(which)

    working = (me == left) | (me == right)
    side_of = lax.div(lax.rem(me - left + lanes, lanes), lanes // 2)

    @pl.when(working)
    def _():
        @pl.loop(0, side // tile)
        def _(t):
            w_ref[at(t), :] = (nn(s_ref[at(t), :], pbuf[...]) + pbuf[at(t), :].astype(F32)).astype(BF16)

        d_ref[...] = tn(w_ref[:, 0:NB], w_ref[:, 0:NB])

        def invert(chunks):
            parts = []
            rounds = diag_rounds(lambda i: d_ref[8 * i : 8 * i + 8, :], lambda i, part: parts.append(part))
            weave(rounds, chunks)
            for i, part in enumerate(parts):
                m_ref[8 * i : 8 * i + 8, :] = part

        def gram(t):
            span = slice(t * tile, (t + 1) * tile)
            a_ref[span, :] = tn(w_ref[:, span], w_ref[...])

        invert([functools.partial(gram, t) for t in range(side // tile)])
        next_diag(0)

        @pl.loop(1, steps)
        def _(step):
            invert(eliminate(step - 1, a_ref, m_ref, lcat, rcat, pair) + product(step - 1))
            next_diag(step)
            send(step - 1)

        mh, ml = halves(m_ref[...])
        scale_row(steps - 1, a_ref, m_ref, mh, ml, rcat, pair)
        for piece in product(steps - 1):
            piece()
        send(steps - 1)

        @pl.loop(0, steps)
        def _(step):
            for turn in range(1, lanes):
                give(side_of, step, turn).wait_send()
            own(side_of, step).wait()

    @pl.when(jnp.logical_not(working))
    def _():
        finish_jobs(jobs)

    for which, worker in enumerate((left, right)):
        @pl.when(me != worker)
        def _():
            @pl.loop(0, steps)
            def _(step):
                give(which, step, 1).wait_recv()


def hand_on(both, first, second):
    first[...] = both[0]
    second[...] = both[1]


def body(grads, row_counts, col_counts, old_left, old_right):
    rows, side = grads.shape[1:]
    lanes = lax.axis_size("tensor")
    steps = side // NB
    vmem = pl.BlockSpec(memory_space=pltpu.VMEM)
    smem = pl.BlockSpec(memory_space=pltpu.SMEM)
    hbm = pl.BlockSpec(memory_space=pl.ANY)
    part = jax.ShapeDtypeStruct((rows, side), BF16)
    dma = pltpu.SemaphoreType.DMA
    whole = pltpu.VMEM((side, side), BF16)
    square = pltpu.VMEM((NB, NB), F32)
    both = pl.pallas_call(
        functools.partial(kernel, lanes),
        out_shape=jax.ShapeDtypeStruct((2, rows, side), BF16),
        in_specs=[smem, smem, vmem, vmem, vmem],
        out_specs=hbm,
        scratch_shapes=[
            pltpu.VMEM((rows, side), BF16),
            whole, whole, whole, whole, whole,
            pltpu.VMEM((side, side), F32),
            pltpu.VMEM((side, 3 * NB), BF16),
            pltpu.VMEM((3 * NB, side), BF16),
            pltpu.VMEM((2 * NB, side), BF16),
            square, square,
            dma((4,)), dma((lanes,)), dma((lanes,)), dma((4,)),
            dma((steps, lanes)), dma((2, steps)), dma((steps,)),
        ],
        compiler_params=pltpu.CompilerParams(
            collective_id=0, has_side_effects=True, vmem_limit_bytes=VMEM_LIMIT
        ),
        cost_estimate=pl.CostEstimate(flops=14 * side**3, bytes_accessed=6 * side * side, transcendentals=0),
        name="refresh",
    )(row_counts, col_counts, grads[0], old_left[0], old_right[0])
    new_left, new_right = pl.pallas_call(
        hand_on,
        out_shape=(part, part),
        in_specs=[vmem],
        out_specs=(vmem, vmem),
        name="hand_on",
    )(both)
    return (new_left[None], new_right[None])


def solution(mesh):
    split = P("fsdp", "tensor", None)
    return jax.shard_map(
        body, mesh=mesh, in_specs=(split, P(), P(), split, split), out_specs=(split, split), check_vma=False
    )
```

```python
import functools

import jax
import jax.numpy as jnp
from jax import lax
from jax.experimental import pallas as pl
from jax.experimental.pallas import tpu as pltpu
from jax.sharding import PartitionSpec as P

MESH = pl.DeviceIdType.MESH
BF16 = jnp.bfloat16
F32 = jnp.float32
NB = 128
VMEM_LIMIT = 56 * 1024 * 1024


def workers(lanes):
    core = lax.rem(lax.axis_index("fsdp"), 2)
    left = core * (lanes // 4)
    return left, left + lanes // 2


def ring_barrier(lanes, me, meanwhile):
    barrier = pltpu.get_barrier_semaphore()
    for step in range(1, lanes):
        other = lax.rem(me + step, lanes)
        pl.semaphore_signal(barrier, inc=1, device_id={"tensor": other}, device_id_type=MESH)
    meanwhile()
    pl.semaphore_wait(barrier, lanes - 1)


def across(column):
    return jnp.broadcast_to(column, (8, NB))


def inverse_rcp(x):
    r = pl.reciprocal(x, approx=True)
    return r * (2.0 - x * r)


def group_update(body, inside, k0, rcp, upper, flat):
    cols = [across(body[:, k0 + q : k0 + q + 1]) for q in range(8)]
    body = jnp.where(inside, 0.0, body)
    for p in range(8):
        w = cols[p] * rcp[p]
        for q in range(p + 1, 8):
            cols[q] = cols[q] - w * upper[p][q]
        body = body - w * flat[p]
    return body


def diag_rounds(load, store):
    count = NB // 8
    sub = lax.broadcasted_iota(jnp.int32, (8, NB), 0)
    lane = lax.broadcasted_iota(jnp.int32, (8, NB), 1)
    rows = [load(i) for i in range(count)]
    for r in range(count):
        k0 = 8 * r
        inside = (lane >= k0) & (lane < k0 + 8)
        top = rows[r]
        cols = [across(top[:, k0 + q : k0 + q + 1]) for q in range(8)]
        u = [{q: across(cols[q][p : p + 1, :]) for q in range(p, 8)} for p in range(8)]
        top = jnp.where(lane - k0 == sub, 1.0, jnp.where(inside, 0.0, top))
        flat = [across(top[p : p + 1, :]) for p in range(8)]
        rcp = [None] * 8
        root = [None] * 8
        for p in range(0, 8, 2):
            n = p + 1
            det = u[p][p] * u[n][n] - u[p][n] * u[p][n]
            rcp[p] = inverse_rcp(u[p][p])
            rcp[n] = u[p][p] * inverse_rcp(det)
            root[p] = lax.rsqrt(u[p][p])
            root[n] = lax.rsqrt(det * rcp[p])
            low = {s: u[p][s] * rcp[p] for s in range(n, 8)}
            for t in range(n + 1, 8):
                u[n][t] = u[n][t] - low[n] * u[p][t]
            high = {s: u[n][s] * rcp[n] for s in range(n + 1, 8)}
            for s in range(n + 1, 8):
                for t in range(s, 8):
                    u[s][t] = u[s][t] - low[s] * u[p][t] - high[s] * u[n][t]
            flat[n] = flat[n] - low[n] * flat[p]
            for s in range(n + 1, 8):
                flat[s] = flat[s] - low[s] * flat[p] - high[s] * flat[n]
        for i in range(r + 1, min(r + 3, count)):
            rows[i] = group_update(rows[i], inside, k0, rcp, u, flat)
        scaled = jnp.zeros((8, NB), F32)
        for p in range(8):
            scaled = jnp.where(sub == p, flat[p] * root[p], scaled)
        store(r, jnp.where(lane <= sub + k0, scaled, 0.0))
        if r + 3 < count:
            high = scaled.astype(BF16).astype(F32)
            low = scaled - high
            zero = jnp.zeros((8, NB), F32)
            left = jnp.concatenate([high, low, high, zero], axis=0).astype(BF16)
            right = jnp.concatenate([high, high, low, zero], axis=0).astype(BF16)
            off = tn(left, right)
            for i in range(r + 3, count):
                rows[i] = jnp.where(inside, 0.0, rows[i]) - off[8 * i : 8 * i + 8, :]
        yield


def weave(rounds, chunks):
    chunks = list(chunks)
    total, rounds_total, given = len(chunks), NB // 8, 0
    for done, _ in enumerate(rounds, 1):
        upto = total * done // rounds_total
        for chunk in chunks[given:upto]:
            chunk()
        given = upto


def halves(x):
    high = x.astype(BF16)
    return high, (x - high.astype(F32)).astype(BF16)


def nt(a, b):
    return lax.dot_general(a, b, (((1,), (1,)), ((), ())), preferred_element_type=F32)


def nn(a, b):
    return jnp.dot(a, b, preferred_element_type=F32)


def tn(a, b):
    return lax.dot_general(a, b, (((0,), (0,)), ((), ())), preferred_element_type=F32)


def eliminate(step, phase, a_ref, m_ref, lcat, rcat, pair):
    side = a_ref.shape[0]
    start = pl.multiple_of(step * NB, NB)
    here = pl.ds(start, NB)
    tile = min(256, side)
    spans = [slice(t * tile, (t + 1) * tile) for t in range(side // tile)]

    def scale():
        mh, ml = halves(m_ref[...])
        scale_row(step, a_ref, m_ref, mh, ml, rcat, pair)

    def multiples(span):
        mh, ml = halves(m_ref[...])
        below = span.start + lax.broadcasted_iota(jnp.int32, (tile, NB), 0) >= start + NB
        column = a_ref[span, here]
        ch, cl = halves(jnp.where(below, column, 0.0))
        low = nt(jnp.concatenate([ch, cl, ch], axis=1), jnp.concatenate([mh, mh, ml], axis=1))
        lh, ll = halves(low)
        lcat[span, 0:NB] = lh
        lcat[span, NB : 2 * NB] = ll
        lcat[span, 2 * NB : 3 * NB] = lh
        a_ref[span, here] = jnp.where(below, 0.0, column)

    def trail(rows, cols):
        a_ref[rows, cols] = a_ref[rows, cols] - nn(lcat[rows, :], rcat[:, cols])

    pieces = [scale] + [functools.partial(multiples, span) for span in spans[phase:]]
    return pieces + [functools.partial(trail, rows, cols) for cols in spans for rows in spans[phase:]]


def scale_row(step, a_ref, m_ref, mh, ml, rcat, pair):
    side = a_ref.shape[0]
    start = pl.multiple_of(step * NB, NB)
    here = pl.ds(start, NB)
    bh, bl = halves(a_ref[here, :])
    fresh = nn(
        jnp.concatenate([mh, ml, mh], axis=1), jnp.concatenate([bh, bh, bl], axis=0)
    )
    a_ref[here, :] = fresh
    a_ref[here, here] = m_ref[...]
    fresh = a_ref[here, :]
    fh, fl = halves(fresh)
    rcat[0:NB, :] = fh
    rcat[NB : 2 * NB, :] = fh
    rcat[2 * NB : 3 * NB, :] = fl
    kept = lax.broadcasted_iota(jnp.int32, (NB, side), 1) < start + NB
    kh, kl = halves(jnp.where(kept, fresh, 0.0))
    pair[0:NB, :] = kh
    pair[NB : 2 * NB, :] = kl


def kernel(
    lanes, rc_ref, cc_ref, g_in, l_in, r_in, out,
    gm, gbuf, pbuf, s_ref, w_ref, x_ref, a_ref, lcat, rcat, pair, m_ref, d_ref,
    ssem, gsem, psem, osem, xsend, xrecv, xown,
):
    me = lax.axis_index("tensor")
    block = lax.axis_index("fsdp")
    rows, side = g_in.shape
    steps = side // NB
    tile = min(256, side)
    left, right = workers(lanes)
    def rows_of(lane):
        return pl.ds(pl.multiple_of(lane * rows, rows), rows)

    mine = rows_of(me)

    def mask():
        rid = me * rows + lax.broadcasted_iota(jnp.int32, (rows, side), 0)
        cid = lax.broadcasted_iota(jnp.int32, (rows, side), 1)
        keep = (rid < rc_ref[block]) & (cid < cc_ref[block])
        gm[...] = jnp.where(keep, g_in[...].astype(F32), 0.0).astype(BF16)

    ring_barrier(lanes, me, mask)

    def remote(src, dst, k, sem, to):
        return pltpu.make_async_remote_copy(
            src_ref=src, dst_ref=dst.at[mine], send_sem=ssem.at[k], recv_sem=sem.at[me],
            device_id={"tensor": to}, device_id_type=MESH,
        )

    jobs = (
        (left, gm, gbuf, 0, gsem), (right, gm, gbuf, 1, gsem), (left, l_in, pbuf, 2, psem), (right, r_in, pbuf, 3, psem)
    )
    for to, src, dst, k, sem in jobs:
        @pl.when(me != to)
        def _():
            remote(src, dst, k, sem, to).start()

        @pl.when(me == to)
        def _():
            pltpu.make_async_copy(src, dst.at[mine], osem.at[k]).start()

    def finish_jobs(chosen):
        for to, src, dst, k, sem in chosen:
            @pl.when(me != to)
            def _():
                remote(src, dst, k, sem, to).wait_send()

            @pl.when(me == to)
            def _():
                pltpu.make_async_copy(src, dst.at[mine], osem.at[k]).wait()

    def arrived(src, dst, sem):
        for step in range(1, lanes):
            other = lax.rem(me + step, lanes)
            pltpu.make_async_remote_copy(
                src_ref=src, dst_ref=dst.at[rows_of(other)], send_sem=ssem.at[0], recv_sem=sem.at[other],
                device_id={"tensor": other}, device_id_type=MESH,
            ).wait_recv()

    def columns(step):
        return pl.ds(pl.multiple_of(step * NB, NB), NB)

    def give(which, step, turn):
        other = lax.rem(me + turn, lanes)
        return pltpu.make_async_remote_copy(
            src_ref=x_ref.at[rows_of(other), columns(step)], dst_ref=out.at[which, :, columns(step)],
            send_sem=xsend.at[step, turn], recv_sem=xrecv.at[which, step],
            device_id={"tensor": other}, device_id_type=MESH,
        )

    def own(which, step):
        return pltpu.make_async_copy(x_ref.at[mine, columns(step)], out.at[which, :, columns(step)], xown.at[step])

    def pair_product(t, depth):
        both = nt(w_ref[t * tile : (t + 1) * tile, :depth], pair[:, :depth])
        return both[:, :NB] + both[:, NB:]

    def product(step, phase):
        def piece(t):
            x_ref[t * tile : (t + 1) * tile, columns(step)] = pair_product(t, tile * (phase + 1)).astype(BF16)

        return [functools.partial(piece, t) for t in range(side // tile)]

    def unscaled_last():
        last = slice(side - NB, side)

        def rows():
            eye = lax.broadcasted_iota(jnp.int32, (NB, NB), 0) == lax.broadcasted_iota(jnp.int32, (NB, NB), 1)
            pair[0:NB, last] = jnp.where(eye, 1.0, 0.0).astype(BF16)
            pair[NB:, last] = jnp.zeros((NB, NB), BF16)
            if side > NB:
                high, low = halves(a_ref[last, : side - NB])
                pair[0:NB, : side - NB] = high
                pair[NB:, : side - NB] = low

        def piece(t):
            span = slice(t * tile, (t + 1) * tile)
            high, low = halves(pair_product(t, side))
            lcat[span, 0:NB] = high
            lcat[span, NB : 2 * NB] = low
            lcat[span, 2 * NB :] = high

        return [rows] + [functools.partial(piece, t) for t in range(side // tile)]

    def send(step):
        for turn in range(1, lanes):
            give(side_of, step, turn).start()
        own(side_of, step).start()

    def at(t):
        return pl.ds(pl.multiple_of(t * tile, tile), tile)

    def next_diag(step):
        later = columns(lax.rem(step + 1, steps))
        mh, ml = halves(m_ref[...])
        ch, cl = halves(a_ref[later, columns(step)])
        low = nt(jnp.concatenate([ch, cl, ch], axis=1), jnp.concatenate([mh, mh, ml], axis=1))
        lh, ll = halves(low)
        d_ref[...] = a_ref[later, later] - nt(
            jnp.concatenate([lh, ll, lh], axis=1), jnp.concatenate([lh, lh, ll], axis=1)
        )

    def begin(which):
        finish_jobs(jobs[which : which + 1])
        arrived(gm, gbuf, gsem)

        @pl.loop(0, side // tile)
        def _(t):
            if which == 0:
                stat = nt(gbuf[at(t), :], gbuf[...])
            else:
                stat = tn(gbuf[:, at(t)], gbuf[...])
            s_ref[at(t), :] = (stat * (1.0 / side)).astype(BF16)

        finish_jobs(jobs[2 + which : 3 + which])
        arrived(l_in, pbuf, psem)
        finish_jobs((jobs[1 - which], jobs[3 - which]))

    for which, worker in enumerate((left, right)):
        @pl.when(me == worker)
        def _():
            begin(which)

    working = (me == left) | (me == right)
    side_of = lax.div(lax.rem(me - left + lanes, lanes), lanes // 2)

    @pl.when(working)
    def _():
        @pl.loop(0, side // tile)
        def _(t):
            w_ref[at(t), :] = (nn(s_ref[at(t), :], pbuf[...]) + pbuf[at(t), :].astype(F32)).astype(BF16)

        d_ref[...] = tn(w_ref[:, 0:NB], w_ref[:, 0:NB])

        def invert(chunks):
            parts = []
            rounds = diag_rounds(lambda i: d_ref[8 * i : 8 * i + 8, :], lambda i, part: parts.append(part))
            weave(rounds, chunks)
            for i, part in enumerate(parts):
                m_ref[8 * i : 8 * i + 8, :] = part

        def gram(t):
            span = slice(t * tile, (t + 1) * tile)
            a_ref[span, :] = tn(w_ref[:, span], w_ref[...])

        invert([functools.partial(gram, t) for t in range(side // tile)])
        next_diag(0)

        each = tile // NB
        for phase in range(side // tile - 1 if side > tile else 0):
            @pl.loop(each * phase + 1, min(each * (phase + 1) + 1, steps - 1))
            def _(step):
                invert(eliminate(step - 1, phase, a_ref, m_ref, lcat, rcat, pair) + product(step - 1, phase))
                next_diag(step)
                send(step - 1)

        phase = side // tile - 1
        last = steps - 1
        invert(
            eliminate(last - 1, phase, a_ref, m_ref, lcat, rcat, pair) + product(last - 1, phase) + unscaled_last()
        )
        send(last - 1)
        mh, ml = halves(m_ref[...])
        for t in range(side // tile):
            span = slice(t * tile, (t + 1) * tile)
            x_ref[span, columns(last)] = nt(lcat[span, :], jnp.concatenate([mh, mh, ml], axis=1)).astype(BF16)
        send(last)

        @pl.loop(0, steps)
        def _(step):
            for turn in range(1, lanes):
                give(side_of, step, turn).wait_send()
            own(side_of, step).wait()

    @pl.when(jnp.logical_not(working))
    def _():
        finish_jobs(jobs)

    for which, worker in enumerate((left, right)):
        @pl.when(me != worker)
        def _():
            @pl.loop(0, steps)
            def _(step):
                give(which, step, 1).wait_recv()


def hand_on(both, first, second):
    first[...] = both[0]
    second[...] = both[1]


def body(grads, row_counts, col_counts, old_left, old_right):
    rows, side = grads.shape[1:]
    lanes = lax.axis_size("tensor")
    steps = side // NB
    vmem = pl.BlockSpec(memory_space=pltpu.VMEM)
    smem = pl.BlockSpec(memory_space=pltpu.SMEM)
    hbm = pl.BlockSpec(memory_space=pl.ANY)
    part = jax.ShapeDtypeStruct((rows, side), BF16)
    dma = pltpu.SemaphoreType.DMA
    whole = pltpu.VMEM((side, side), BF16)
    square = pltpu.VMEM((NB, NB), F32)
    both = pl.pallas_call(
        functools.partial(kernel, lanes),
        out_shape=jax.ShapeDtypeStruct((2, rows, side), BF16),
        in_specs=[smem, smem, vmem, vmem, vmem],
        out_specs=hbm,
        scratch_shapes=[
            pltpu.VMEM((rows, side), BF16),
            whole, whole, whole, whole, whole,
            pltpu.VMEM((side, side), F32),
            pltpu.VMEM((side, 3 * NB), BF16),
            pltpu.VMEM((3 * NB, side), BF16),
            pltpu.VMEM((2 * NB, side), BF16),
            square, square,
            dma((4,)), dma((lanes,)), dma((lanes,)), dma((4,)),
            dma((steps, lanes)), dma((2, steps)), dma((steps,)),
        ],
        compiler_params=pltpu.CompilerParams(
            collective_id=0, has_side_effects=True, vmem_limit_bytes=VMEM_LIMIT
        ),
        cost_estimate=pl.CostEstimate(flops=14 * side**3, bytes_accessed=6 * side * side, transcendentals=0),
        name="refresh",
    )(row_counts, col_counts, grads[0], old_left[0], old_right[0])
    new_left, new_right = pl.pallas_call(
        hand_on,
        out_shape=(part, part),
        in_specs=[vmem],
        out_specs=(vmem, vmem),
        name="hand_on",
    )(both)
    return (new_left[None], new_right[None])


def solution(mesh):
    split = P("fsdp", "tensor", None)
    return jax.shard_map(
        body, mesh=mesh, in_specs=(split, P(), P(), split, split), out_specs=(split, split), check_vma=False
    )
```

```python
import functools

import jax
import jax.numpy as jnp
from jax import lax
from jax.experimental import pallas as pl
from jax.experimental.pallas import tpu as pltpu
from jax.sharding import PartitionSpec as P

MESH = pl.DeviceIdType.MESH
BF16 = jnp.bfloat16
F32 = jnp.float32
NB = 128
NEAR = 3
VMEM_LIMIT = 56 * 1024 * 1024


def workers(lanes):
    core = lax.rem(lax.axis_index("fsdp"), 2)
    left = core * (lanes // 4)
    return left, left + lanes // 2


def ring_barrier(lanes, me, meanwhile):
    barrier = pltpu.get_barrier_semaphore()
    for step in range(1, lanes):
        other = lax.rem(me + step, lanes)
        pl.semaphore_signal(barrier, inc=1, device_id={"tensor": other}, device_id_type=MESH)
    meanwhile()
    pl.semaphore_wait(barrier, lanes - 1)


def across(column):
    return jnp.broadcast_to(column, (8, NB))


def inverse_rcp(x):
    r = pl.reciprocal(x, approx=True)
    return r * (2.0 - x * r)


def group_update(body, inside, k0, rcp, upper, flat):
    cols = [across(body[:, k0 + q : k0 + q + 1]) for q in range(8)]
    body = jnp.where(inside, 0.0, body)
    for p in range(8):
        w = cols[p] * rcp[p]
        for q in range(p + 1, 8):
            cols[q] = cols[q] - w * upper[p][q]
        body = body - w * flat[p]
    return body


def diag_rounds(load, store, lines):
    count = NB // 8
    sub = lax.broadcasted_iota(jnp.int32, (8, NB), 0)
    lane = lax.broadcasted_iota(jnp.int32, (8, NB), 1)
    rows = [load(i) for i in range(count)]
    for r in range(count):
        k0 = 8 * r
        inside = (lane >= k0) & (lane < k0 + 8)
        lines[8 * r : 8 * r + 8, :] = rows[r]
        flat = [across(lines[k0 + p : k0 + p + 1, :]) for p in range(8)]
        u = [{q: across(flat[p][:, k0 + q : k0 + q + 1]) for q in range(p, 8)} for p in range(8)]
        flat = [jnp.where(lane == k0 + p, 1.0, jnp.where(inside, 0.0, flat[p])) for p in range(8)]
        rcp = [None] * 8
        root = [None] * 8
        for p in range(0, 8, 2):
            n = p + 1
            a, b, c = u[p][p], u[p][n], u[n][n]
            det = a * c - b * b
            guess = pl.reciprocal(det, approx=True)
            fix = 2.0 - det * guess
            for s in range(n + 1, 8):
                g = c * u[p][s] - b * u[n][s]
                h = a * u[n][s] - b * u[p][s]
                for t in range(s, 8):
                    u[s][t] = u[s][t] - ((g * u[p][t] + h * u[n][t]) * guess) * fix
            rcp[p] = inverse_rcp(a)
            rcp[n] = a * (guess * fix)
            root[p] = lax.rsqrt(a)
            root[n] = lax.rsqrt(det * rcp[p])
            low = {s: u[p][s] * rcp[p] for s in range(n, 8)}
            for t in range(n + 1, 8):
                u[n][t] = u[n][t] - low[n] * u[p][t]
            flat[n] = flat[n] - low[n] * flat[p]
            for s in range(n + 1, 8):
                flat[s] = flat[s] - low[s] * flat[p] - (u[n][s] * rcp[n]) * flat[n]
        for i in range(r + 1, min(r + 1 + NEAR, count)):
            rows[i] = group_update(rows[i], inside, k0, rcp, u, flat)
        scaled = jnp.zeros((8, NB), F32)
        for p in range(8):
            scaled = jnp.where(sub == p, flat[p] * root[p], scaled)
        store(r, jnp.where(lane <= sub + k0, scaled, 0.0))
        if r + 1 + NEAR < count:
            high = scaled.astype(BF16).astype(F32)
            low = scaled - high
            zero = jnp.zeros((8, NB), F32)
            left = jnp.concatenate([high, low, high, zero], axis=0).astype(BF16)
            right = jnp.concatenate([high, high, low, zero], axis=0).astype(BF16)
            off = tn(left, right)
            for i in range(r + 1 + NEAR, count):
                rows[i] = jnp.where(inside, 0.0, rows[i]) - off[8 * i : 8 * i + 8, :]
        yield


def weave(rounds, chunks):
    chunks = list(chunks)
    total, rounds_total, given = len(chunks), NB // 8, 0
    for done, _ in enumerate(rounds, 1):
        upto = total * done // rounds_total
        for chunk in chunks[given:upto]:
            chunk()
        given = upto


def halves(x):
    high = x.astype(BF16)
    return high, (x - high.astype(F32)).astype(BF16)


def nt(a, b):
    return lax.dot_general(a, b, (((1,), (1,)), ((), ())), preferred_element_type=F32)


def nn(a, b):
    return jnp.dot(a, b, preferred_element_type=F32)


def tn(a, b):
    return lax.dot_general(a, b, (((0,), (0,)), ((), ())), preferred_element_type=F32)


def eliminate(step, phase, a_ref, m_ref, lcat, rcat, pair):
    side = a_ref.shape[0]
    start = pl.multiple_of(step * NB, NB)
    here = pl.ds(start, NB)
    tile = min(256, side)
    spans = [slice(t * tile, (t + 1) * tile) for t in range(side // tile)]

    def scale():
        mh, ml = halves(m_ref[...])
        scale_row(step, a_ref, m_ref, mh, ml, rcat, pair)

    def multiples(span):
        mh, ml = halves(m_ref[...])
        below = span.start + lax.broadcasted_iota(jnp.int32, (tile, NB), 0) >= start + NB
        column = a_ref[span, here]
        ch, cl = halves(jnp.where(below, column, 0.0))
        low = nt(jnp.concatenate([ch, cl, ch], axis=1), jnp.concatenate([mh, mh, ml], axis=1))
        lh, ll = halves(low)
        lcat[span, 0:NB] = lh
        lcat[span, NB : 2 * NB] = ll
        lcat[span, 2 * NB : 3 * NB] = lh
        a_ref[span, here] = jnp.where(below, 0.0, column)

    def trail(rows, cols):
        a_ref[rows, cols] = a_ref[rows, cols] - nn(lcat[rows, :], rcat[:, cols])

    pieces = [scale] + [functools.partial(multiples, span) for span in spans[phase:]]
    return pieces + [functools.partial(trail, rows, cols) for cols in spans for rows in spans[phase:]]


def scale_row(step, a_ref, m_ref, mh, ml, rcat, pair):
    side = a_ref.shape[0]
    start = pl.multiple_of(step * NB, NB)
    here = pl.ds(start, NB)
    bh, bl = halves(a_ref[here, :])
    fresh = nn(
        jnp.concatenate([mh, ml, mh], axis=1), jnp.concatenate([bh, bh, bl], axis=0)
    )
    a_ref[here, :] = fresh
    a_ref[here, here] = m_ref[...]
    fresh = a_ref[here, :]
    fh, fl = halves(fresh)
    rcat[0:NB, :] = fh
    rcat[NB : 2 * NB, :] = fh
    rcat[2 * NB : 3 * NB, :] = fl
    kept = lax.broadcasted_iota(jnp.int32, (NB, side), 1) < start + NB
    kh, kl = halves(jnp.where(kept, fresh, 0.0))
    pair[0:NB, :] = kh
    pair[NB : 2 * NB, :] = kl


def kernel(
    lanes, rc_ref, cc_ref, g_in, l_in, r_in, out,
    gm, gbuf, pbuf, s_ref, w_ref, x_ref, a_ref, lcat, rcat, pair, m_ref, d_ref, lines,
    ssem, gsem, psem, osem, xsend, xrecv, xown,
):
    me = lax.axis_index("tensor")
    block = lax.axis_index("fsdp")
    rows, side = g_in.shape
    steps = side // NB
    tile = min(256, side)
    left, right = workers(lanes)
    def rows_of(lane):
        return pl.ds(pl.multiple_of(lane * rows, rows), rows)

    mine = rows_of(me)

    def mask():
        rid = me * rows + lax.broadcasted_iota(jnp.int32, (rows, side), 0)
        cid = lax.broadcasted_iota(jnp.int32, (rows, side), 1)
        keep = (rid < rc_ref[block]) & (cid < cc_ref[block])
        gm[...] = jnp.where(keep, g_in[...].astype(F32), 0.0).astype(BF16)

    ring_barrier(lanes, me, mask)

    def remote(src, dst, k, sem, to):
        return pltpu.make_async_remote_copy(
            src_ref=src, dst_ref=dst.at[mine], send_sem=ssem.at[k], recv_sem=sem.at[me],
            device_id={"tensor": to}, device_id_type=MESH,
        )

    jobs = (
        (left, gm, gbuf, 0, gsem), (right, gm, gbuf, 1, gsem), (left, l_in, pbuf, 2, psem), (right, r_in, pbuf, 3, psem)
    )
    for to, src, dst, k, sem in jobs:
        @pl.when(me != to)
        def _():
            remote(src, dst, k, sem, to).start()

        @pl.when(me == to)
        def _():
            pltpu.make_async_copy(src, dst.at[mine], osem.at[k]).start()

    def finish_jobs(chosen):
        for to, src, dst, k, sem in chosen:
            @pl.when(me != to)
            def _():
                remote(src, dst, k, sem, to).wait_send()

            @pl.when(me == to)
            def _():
                pltpu.make_async_copy(src, dst.at[mine], osem.at[k]).wait()

    def arrived(src, dst, sem):
        for step in range(1, lanes):
            other = lax.rem(me + step, lanes)
            pltpu.make_async_remote_copy(
                src_ref=src, dst_ref=dst.at[rows_of(other)], send_sem=ssem.at[0], recv_sem=sem.at[other],
                device_id={"tensor": other}, device_id_type=MESH,
            ).wait_recv()

    def columns(step):
        return pl.ds(pl.multiple_of(step * NB, NB), NB)

    def give(which, step, turn):
        other = lax.rem(me + turn, lanes)
        return pltpu.make_async_remote_copy(
            src_ref=x_ref.at[rows_of(other), columns(step)], dst_ref=out.at[which, :, columns(step)],
            send_sem=xsend.at[step, turn], recv_sem=xrecv.at[which, step],
            device_id={"tensor": other}, device_id_type=MESH,
        )

    def own(which, step):
        return pltpu.make_async_copy(x_ref.at[mine, columns(step)], out.at[which, :, columns(step)], xown.at[step])

    def pair_product(t, depth):
        both = nt(w_ref[t * tile : (t + 1) * tile, :depth], pair[:, :depth])
        return both[:, :NB] + both[:, NB:]

    def product(step, phase):
        def piece(t):
            x_ref[t * tile : (t + 1) * tile, columns(step)] = pair_product(t, tile * (phase + 1)).astype(BF16)

        return [functools.partial(piece, t) for t in range(side // tile)]

    def unscaled_last():
        last = slice(side - NB, side)

        def rows():
            eye = lax.broadcasted_iota(jnp.int32, (NB, NB), 0) == lax.broadcasted_iota(jnp.int32, (NB, NB), 1)
            pair[0:NB, last] = jnp.where(eye, 1.0, 0.0).astype(BF16)
            pair[NB:, last] = jnp.zeros((NB, NB), BF16)
            if side > NB:
                high, low = halves(a_ref[last, : side - NB])
                pair[0:NB, : side - NB] = high
                pair[NB:, : side - NB] = low

        def piece(t):
            span = slice(t * tile, (t + 1) * tile)
            high, low = halves(pair_product(t, side))
            lcat[span, 0:NB] = high
            lcat[span, NB : 2 * NB] = low
            lcat[span, 2 * NB :] = high

        return [rows] + [functools.partial(piece, t) for t in range(side // tile)]

    def send(step):
        for turn in range(1, lanes):
            give(side_of, step, turn).start()
        own(side_of, step).start()

    def at(t):
        return pl.ds(pl.multiple_of(t * tile, tile), tile)

    def next_diag(step):
        later = columns(lax.rem(step + 1, steps))
        mh, ml = halves(m_ref[...])
        ch, cl = halves(a_ref[later, columns(step)])
        low = nt(jnp.concatenate([ch, cl, ch], axis=1), jnp.concatenate([mh, mh, ml], axis=1))
        lh, ll = halves(low)
        d_ref[...] = a_ref[later, later] - nt(
            jnp.concatenate([lh, ll, lh], axis=1), jnp.concatenate([lh, lh, ll], axis=1)
        )

    def begin(which):
        finish_jobs(jobs[which : which + 1])
        arrived(gm, gbuf, gsem)

        @pl.loop(0, side // tile)
        def _(t):
            if which == 0:
                stat = nt(gbuf[at(t), :], gbuf[...])
            else:
                stat = tn(gbuf[:, at(t)], gbuf[...])
            s_ref[at(t), :] = (stat * (1.0 / side)).astype(BF16)

        finish_jobs(jobs[2 + which : 3 + which])
        arrived(l_in, pbuf, psem)
        finish_jobs((jobs[1 - which], jobs[3 - which]))

    for which, worker in enumerate((left, right)):
        @pl.when(me == worker)
        def _():
            begin(which)

    working = (me == left) | (me == right)
    side_of = lax.div(lax.rem(me - left + lanes, lanes), lanes // 2)

    @pl.when(working)
    def _():
        @pl.loop(0, side // tile)
        def _(t):
            w_ref[at(t), :] = (nn(s_ref[at(t), :], pbuf[...]) + pbuf[at(t), :].astype(F32)).astype(BF16)

        d_ref[...] = tn(w_ref[:, 0:NB], w_ref[:, 0:NB])

        def invert(chunks):
            parts = []
            rounds = diag_rounds(lambda i: d_ref[8 * i : 8 * i + 8, :], lambda i, part: parts.append(part), lines)
            weave(rounds, chunks)
            for i, part in enumerate(parts):
                m_ref[8 * i : 8 * i + 8, :] = part

        def gram(t):
            span = slice(t * tile, (t + 1) * tile)
            a_ref[span, :] = tn(w_ref[:, span], w_ref[...])

        invert([functools.partial(gram, t) for t in range(side // tile)])
        next_diag(0)

        each = tile // NB
        for phase in range(side // tile - 1 if side > tile else 0):
            @pl.loop(each * phase + 1, min(each * (phase + 1) + 1, steps - 1))
            def _(step):
                invert(eliminate(step - 1, phase, a_ref, m_ref, lcat, rcat, pair) + product(step - 1, phase))
                next_diag(step)
                send(step - 1)

        phase = side // tile - 1
        last = steps - 1
        invert(
            eliminate(last - 1, phase, a_ref, m_ref, lcat, rcat, pair) + product(last - 1, phase) + unscaled_last()
        )
        send(last - 1)
        mh, ml = halves(m_ref[...])
        for t in range(side // tile):
            span = slice(t * tile, (t + 1) * tile)
            x_ref[span, columns(last)] = nt(lcat[span, :], jnp.concatenate([mh, mh, ml], axis=1)).astype(BF16)
        send(last)

        @pl.loop(0, steps)
        def _(step):
            for turn in range(1, lanes):
                give(side_of, step, turn).wait_send()
            own(side_of, step).wait()

    @pl.when(jnp.logical_not(working))
    def _():
        finish_jobs(jobs)

    for which, worker in enumerate((left, right)):
        @pl.when(me != worker)
        def _():
            @pl.loop(0, steps)
            def _(step):
                give(which, step, 1).wait_recv()


def hand_on(both, first, second):
    first[...] = both[0]
    second[...] = both[1]


def body(grads, row_counts, col_counts, old_left, old_right):
    rows, side = grads.shape[1:]
    lanes = lax.axis_size("tensor")
    steps = side // NB
    vmem = pl.BlockSpec(memory_space=pltpu.VMEM)
    smem = pl.BlockSpec(memory_space=pltpu.SMEM)
    hbm = pl.BlockSpec(memory_space=pl.ANY)
    part = jax.ShapeDtypeStruct((rows, side), BF16)
    dma = pltpu.SemaphoreType.DMA
    whole = pltpu.VMEM((side, side), BF16)
    square = pltpu.VMEM((NB, NB), F32)
    both = pl.pallas_call(
        functools.partial(kernel, lanes),
        out_shape=jax.ShapeDtypeStruct((2, rows, side), BF16),
        in_specs=[smem, smem, vmem, vmem, vmem],
        out_specs=hbm,
        scratch_shapes=[
            pltpu.VMEM((rows, side), BF16),
            whole, whole, whole, whole, whole,
            pltpu.VMEM((side, side), F32),
            pltpu.VMEM((side, 3 * NB), BF16),
            pltpu.VMEM((3 * NB, side), BF16),
            pltpu.VMEM((2 * NB, side), BF16),
            square, square, square,
            dma((4,)), dma((lanes,)), dma((lanes,)), dma((4,)),
            dma((steps, lanes)), dma((2, steps)), dma((steps,)),
        ],
        compiler_params=pltpu.CompilerParams(
            collective_id=0, has_side_effects=True, vmem_limit_bytes=VMEM_LIMIT
        ),
        cost_estimate=pl.CostEstimate(flops=14 * side**3, bytes_accessed=6 * side * side, transcendentals=0),
        name="refresh",
    )(row_counts, col_counts, grads[0], old_left[0], old_right[0])
    new_left, new_right = pl.pallas_call(
        hand_on,
        out_shape=(part, part),
        in_specs=[vmem],
        out_specs=(vmem, vmem),
        name="hand_on",
    )(both)
    return (new_left[None], new_right[None])


def solution(mesh):
    split = P("fsdp", "tensor", None)
    return jax.shard_map(
        body, mesh=mesh, in_specs=(split, P(), P(), split, split), out_specs=(split, split), check_vma=False
    )
```

```python
import functools

import jax
import jax.numpy as jnp
from jax import lax
from jax.experimental import pallas as pl
from jax.experimental.pallas import tpu as pltpu
from jax.sharding import PartitionSpec as P

MESH = pl.DeviceIdType.MESH
BF16 = jnp.bfloat16
F32 = jnp.float32
NB = 128
PANEL = 32
VMEM_LIMIT = 56 * 1024 * 1024


def workers(lanes):
    core = lax.rem(lax.axis_index("fsdp"), 2)
    left = core * (lanes // 4)
    return left, left + lanes // 2


def ring_barrier(lanes, me, meanwhile):
    barrier = pltpu.get_barrier_semaphore()
    for step in range(1, lanes):
        other = lax.rem(me + step, lanes)
        pl.semaphore_signal(barrier, inc=1, device_id={"tensor": other}, device_id_type=MESH)
    meanwhile()
    pl.semaphore_wait(barrier, lanes - 1)


def across(column):
    return jnp.broadcast_to(column, (8, NB))


def inverse_rcp(x):
    r = pl.reciprocal(x, approx=True)
    return r * (2.0 - x * r)


def group_update(body, inside, k0, rcp, upper, flat):
    cols = [across(body[:, k0 + q : k0 + q + 1]) for q in range(8)]
    body = jnp.where(inside, 0.0, body)
    for p in range(8):
        w = cols[p] * rcp[p]
        for q in range(p + 1, 8):
            cols[q] = cols[q] - w * upper[p][q]
        body = body - w * flat[p]
    return body


def panel_rounds(turn, q_ref):
    groups, panel = NB // 8, PANEL // 8
    sub = lax.broadcasted_iota(jnp.int32, (8, NB), 0)
    lane = lax.broadcasted_iota(jnp.int32, (8, NB), 1)
    rows = [q_ref[8 * i : 8 * i + 8, :] for i in range(panel)]
    done = []
    for r in range(panel):
        k0 = 8 * r
        inside = (lane >= k0) & (lane < k0 + 8)
        flat = [across(rows[r][p : p + 1, :]) for p in range(8)]
        cols = [across(rows[r][:, k0 + q : k0 + q + 1]) for q in range(8)]
        u = [{q: across(cols[q][p : p + 1, :]) for q in range(p, 8)} for p in range(8)]
        flat = [jnp.where(lane == k0 + p, 1.0, jnp.where(inside, 0.0, flat[p])) for p in range(8)]
        rcp = [None] * 8
        root = [None] * 8
        for p in range(0, 8, 2):
            n = p + 1
            a, b, c = u[p][p], u[p][n], u[n][n]
            det = a * c - b * b
            guess = pl.reciprocal(det, approx=True)
            fix = 2.0 - det * guess
            for s in range(n + 1, 8):
                g = c * u[p][s] - b * u[n][s]
                h = a * u[n][s] - b * u[p][s]
                for t in range(s, 8):
                    u[s][t] = u[s][t] - ((g * u[p][t] + h * u[n][t]) * guess) * fix
            rcp[p] = inverse_rcp(a)
            rcp[n] = a * (guess * fix)
            root[p] = lax.rsqrt(a)
            root[n] = lax.rsqrt(det * rcp[p])
            low = {s: u[p][s] * rcp[p] for s in range(n, 8)}
            for t in range(n + 1, 8):
                u[n][t] = u[n][t] - low[n] * u[p][t]
            flat[n] = flat[n] - low[n] * flat[p]
            for s in range(n + 1, 8):
                flat[s] = flat[s] - low[s] * flat[p] - (u[n][s] * rcp[n]) * flat[n]
        for i in range(r + 1, panel):
            rows[i] = group_update(rows[i], inside, k0, rcp, u, flat)
        scaled = jnp.zeros((8, NB), F32)
        for p in range(8):
            scaled = jnp.where(sub == p, flat[p] * root[p], scaled)
        done.append(jnp.where((lane < PANEL) & (lane > sub + k0), 0.0, scaled))
        yield
    whole = jnp.concatenate(done, axis=0)
    high = whole.astype(BF16).astype(F32)
    low = whole - high
    ahead = lax.broadcasted_iota(jnp.int32, (PANEL, NB), 1)
    ahead = (ahead >= PANEL) & (ahead < NB - PANEL * turn)
    left = jnp.concatenate([high, low, high], axis=0)
    ahead = jnp.concatenate([ahead.astype(F32)] * 3, axis=0)
    left = (left * ahead).astype(BF16)
    right = jnp.concatenate([high, high, low], axis=0).astype(BF16)
    off = tn(left, right)
    for i in range(panel, groups):
        rest = jnp.where(lane < PANEL, 0.0, q_ref[8 * i : 8 * i + 8, :]) - off[8 * i : 8 * i + 8, :]
        q_ref[8 * (i - panel) : 8 * (i - panel) + 8, :] = pltpu.roll(rest, NB - PANEL, 1)
    for r in range(panel):
        place = groups - panel + r
        q_ref[8 * place : 8 * place + 8, :] = pltpu.roll(done[r], NB - PANEL, 1)


def weave(rounds, chunks):
    total, rounds_total, given = len(chunks), PANEL // 8, 0
    for done, _ in enumerate(rounds, 1):
        upto = total * done // rounds_total
        for chunk in chunks[given:upto]:
            chunk()
        given = upto


def halves(x):
    high = x.astype(BF16)
    return high, (x - high.astype(F32)).astype(BF16)


def nt(a, b):
    return lax.dot_general(a, b, (((1,), (1,)), ((), ())), preferred_element_type=F32)


def nn(a, b):
    return jnp.dot(a, b, preferred_element_type=F32)


def tn(a, b):
    return lax.dot_general(a, b, (((0,), (0,)), ((), ())), preferred_element_type=F32)


def scale_step(step, phase, a_ref, m_ref, lcat, rcat, pair):
    side = a_ref.shape[0]
    start = pl.multiple_of(step * NB, NB)
    here = pl.ds(start, NB)
    tile = min(256, side)
    span = slice(phase * tile, side)
    mh, ml = halves(m_ref[...])
    scale_row(step, a_ref, m_ref, mh, ml, rcat, pair)
    below = phase * tile + lax.broadcasted_iota(jnp.int32, (side - phase * tile, NB), 0) >= start + NB
    column = a_ref[span, here]
    ch, cl = halves(jnp.where(below, column, 0.0))
    low = nt(jnp.concatenate([ch, cl, ch], axis=1), jnp.concatenate([mh, mh, ml], axis=1))
    lh, ll = halves(low)
    lcat[span, 0:NB] = lh
    lcat[span, NB : 2 * NB] = ll
    lcat[span, 2 * NB : 3 * NB] = lh
    a_ref[span, here] = jnp.where(below, 0.0, column)


def scale_row(step, a_ref, m_ref, mh, ml, rcat, pair):
    side = a_ref.shape[0]
    start = pl.multiple_of(step * NB, NB)
    here = pl.ds(start, NB)
    bh, bl = halves(a_ref[here, :])
    fresh = nn(
        jnp.concatenate([mh, ml, mh], axis=1), jnp.concatenate([bh, bh, bl], axis=0)
    )
    a_ref[here, :] = fresh
    a_ref[here, here] = m_ref[...]
    fresh = a_ref[here, :]
    fh, fl = halves(fresh)
    rcat[0:NB, :] = fh
    rcat[NB : 2 * NB, :] = fh
    rcat[2 * NB : 3 * NB, :] = fl
    kept = lax.broadcasted_iota(jnp.int32, (NB, side), 1) < start + NB
    kh, kl = halves(jnp.where(kept, fresh, 0.0))
    pair[0:NB, :] = kh
    pair[NB : 2 * NB, :] = kl


def kernel(
    lanes, rc_ref, cc_ref, g_in, l_in, r_in, out,
    gm, gbuf, pbuf, s_ref, w_ref, x_ref, a_ref, lcat, rcat, pair, pair2, m_ref, d_ref,
    ssem, gsem, psem, osem, xsend, xrecv, xown,
):
    me = lax.axis_index("tensor")
    block = lax.axis_index("fsdp")
    rows, side = g_in.shape
    steps = side // NB
    tile = min(256, side)
    left, right = workers(lanes)
    def rows_of(lane):
        return pl.ds(pl.multiple_of(lane * rows, rows), rows)

    mine = rows_of(me)

    def mask():
        rid = me * rows + lax.broadcasted_iota(jnp.int32, (rows, side), 0)
        cid = lax.broadcasted_iota(jnp.int32, (rows, side), 1)
        keep = (rid < rc_ref[block]) & (cid < cc_ref[block])
        gm[...] = jnp.where(keep, g_in[...].astype(F32), 0.0).astype(BF16)

    ring_barrier(lanes, me, mask)

    def remote(src, dst, k, sem, to):
        return pltpu.make_async_remote_copy(
            src_ref=src, dst_ref=dst.at[mine], send_sem=ssem.at[k], recv_sem=sem.at[me],
            device_id={"tensor": to}, device_id_type=MESH,
        )

    jobs = (
        (left, gm, gbuf, 0, gsem), (right, gm, gbuf, 1, gsem), (left, l_in, pbuf, 2, psem), (right, r_in, pbuf, 3, psem)
    )
    for to, src, dst, k, sem in jobs:
        @pl.when(me != to)
        def _():
            remote(src, dst, k, sem, to).start()

        @pl.when(me == to)
        def _():
            pltpu.make_async_copy(src, dst.at[mine], osem.at[k]).start()

    def finish_jobs(chosen):
        for to, src, dst, k, sem in chosen:
            @pl.when(me != to)
            def _():
                remote(src, dst, k, sem, to).wait_send()

            @pl.when(me == to)
            def _():
                pltpu.make_async_copy(src, dst.at[mine], osem.at[k]).wait()

    def arrived(src, dst, sem):
        for step in range(1, lanes):
            other = lax.rem(me + step, lanes)
            pltpu.make_async_remote_copy(
                src_ref=src, dst_ref=dst.at[rows_of(other)], send_sem=ssem.at[0], recv_sem=sem.at[other],
                device_id={"tensor": other}, device_id_type=MESH,
            ).wait_recv()

    def columns(step):
        return pl.ds(pl.multiple_of(step * NB, NB), NB)

    def give(which, step, turn):
        other = lax.rem(me + turn, lanes)
        return pltpu.make_async_remote_copy(
            src_ref=x_ref.at[rows_of(other), columns(step)], dst_ref=out.at[which, :, columns(step)],
            send_sem=xsend.at[step, turn], recv_sem=xrecv.at[which, step],
            device_id={"tensor": other}, device_id_type=MESH,
        )

    def own(which, step):
        return pltpu.make_async_copy(x_ref.at[mine, columns(step)], out.at[which, :, columns(step)], xown.at[step])

    def at(t):
        return pl.ds(pl.multiple_of(t * tile, tile), tile)

    def pair_product(t, depth, rows):
        both = nt(w_ref[at(t), :depth], rows[:, :depth])
        return both[:, :NB] + both[:, NB:]

    def product(t, step, phase):
        x_ref[at(t), columns(step)] = pair_product(t, tile * (phase + 1), pair).astype(BF16)

    def trail(t, first):
        rows = slice(first * tile, (first + 1) * tile)
        a_ref[rows, at(t)] = a_ref[rows, at(t)] - nn(lcat[rows, :], rcat[:, at(t)])

    def last_rows():
        last = slice(side - NB, side)
        eye = lax.broadcasted_iota(jnp.int32, (NB, NB), 0) == lax.broadcasted_iota(jnp.int32, (NB, NB), 1)
        pair2[0:NB, last] = jnp.where(eye, 1.0, 0.0).astype(BF16)
        pair2[NB:, last] = jnp.zeros((NB, NB), BF16)
        high, low = halves(a_ref[last, : side - NB])
        pair2[0:NB, : side - NB] = high
        pair2[NB:, : side - NB] = low

    def unscaled(t):
        high, low = halves(pair_product(t, side, pair2))
        lcat[at(t), 0:NB] = high
        lcat[at(t), NB : 2 * NB] = low
        lcat[at(t), 2 * NB :] = high

    def send(step):
        for turn in range(1, lanes):
            give(side_of, step, turn).start()
        own(side_of, step).start()

    def next_diag(step):
        later = columns(lax.rem(step + 1, steps))
        mh, ml = halves(m_ref[...])
        ch, cl = halves(a_ref[later, columns(step)])
        low = nt(jnp.concatenate([ch, cl, ch], axis=1), jnp.concatenate([mh, mh, ml], axis=1))
        lh, ll = halves(low)
        d_ref[...] = a_ref[later, later] - nt(
            jnp.concatenate([lh, ll, lh], axis=1), jnp.concatenate([lh, lh, ll], axis=1)
        )

    def begin(which):
        finish_jobs(jobs[which : which + 1])
        arrived(gm, gbuf, gsem)

        @pl.loop(0, side // tile)
        def _(t):
            if which == 0:
                stat = nt(gbuf[at(t), :], gbuf[...])
            else:
                stat = tn(gbuf[:, at(t)], gbuf[...])
            s_ref[at(t), :] = (stat * (1.0 / side)).astype(BF16)

        finish_jobs(jobs[2 + which : 3 + which])
        arrived(l_in, pbuf, psem)
        finish_jobs((jobs[1 - which], jobs[3 - which]))

    for which, worker in enumerate((left, right)):
        @pl.when(me == worker)
        def _():
            begin(which)

    working = (me == left) | (me == right)
    side_of = lax.div(lax.rem(me - left + lanes, lanes), lanes // 2)

    @pl.when(working)
    def _():
        @pl.loop(0, side // tile)
        def _(t):
            w_ref[at(t), :] = (nn(s_ref[at(t), :], pbuf[...]) + pbuf[at(t), :].astype(F32)).astype(BF16)

        d_ref[...] = tn(w_ref[:, 0:NB], w_ref[:, 0:NB])

        def invert(chunks):
            @pl.loop(0, NB // PANEL)
            def _(t):
                weave(panel_rounds(t, d_ref), chunks(t))

            lower = lax.broadcasted_iota(jnp.int32, (NB, NB), 1) <= lax.broadcasted_iota(jnp.int32, (NB, NB), 0)
            m_ref[...] = jnp.where(lower, d_ref[...], 0.0)

        def some(count, work):
            if count == NB // PANEL:
                return lambda t: [functools.partial(work, t)]

            def only(t):
                @pl.when(t == 0)
                def _():
                    for k in range(count):
                        work(k)

            return lambda t: [functools.partial(only, t)]

        def gram(t):
            a_ref[at(t), :] = tn(w_ref[:, at(t)], w_ref[...])

        tiles = side // tile
        each = tile // NB
        invert(some(tiles, gram))
        next_diag(0)
        scale_step(0, 0, a_ref, m_ref, lcat, rcat, pair)

        def update(t, step, phase):
            for first in range(phase, tiles):
                trail(t, first)
            product(t, step, phase)

        for phase in range(tiles):
            if each * phase + 1 < min(each * (phase + 1) + 1, steps - 1):
                @pl.loop(each * phase + 1, min(each * (phase + 1) + 1, steps - 1))
                def _(step):
                    invert(some(tiles, functools.partial(update, step=step - 1, phase=phase)))
                    next_diag(step)
                    scale_step(step, phase, a_ref, m_ref, lcat, rcat, pair)
                    send(step - 1)

        phase = tiles - 1
        last = steps - 1

        @pl.loop(0, tiles)
        def _(t):
            trail(t, phase)

        last_rows()

        def finish(t):
            product(t, last - 1, phase)
            unscaled(t)

        invert(some(tiles, finish))
        send(last - 1)
        mh, ml = halves(m_ref[...])
        for t in range(tiles):
            span = slice(t * tile, (t + 1) * tile)
            x_ref[span, columns(last)] = nt(lcat[span, :], jnp.concatenate([mh, mh, ml], axis=1)).astype(BF16)
        send(last)

        @pl.loop(0, steps)
        def _(step):
            for turn in range(1, lanes):
                give(side_of, step, turn).wait_send()
            own(side_of, step).wait()

    @pl.when(jnp.logical_not(working))
    def _():
        finish_jobs(jobs)

    for which, worker in enumerate((left, right)):
        @pl.when(me != worker)
        def _():
            @pl.loop(0, steps)
            def _(step):
                give(which, step, 1).wait_recv()


def hand_on(both, first, second):
    first[...] = both[0]
    second[...] = both[1]


def body(grads, row_counts, col_counts, old_left, old_right):
    rows, side = grads.shape[1:]
    lanes = lax.axis_size("tensor")
    steps = side // NB
    vmem = pl.BlockSpec(memory_space=pltpu.VMEM)
    smem = pl.BlockSpec(memory_space=pltpu.SMEM)
    hbm = pl.BlockSpec(memory_space=pl.ANY)
    part = jax.ShapeDtypeStruct((rows, side), BF16)
    dma = pltpu.SemaphoreType.DMA
    whole = pltpu.VMEM((side, side), BF16)
    square = pltpu.VMEM((NB, NB), F32)
    both = pl.pallas_call(
        functools.partial(kernel, lanes),
        out_shape=jax.ShapeDtypeStruct((2, rows, side), BF16),
        in_specs=[smem, smem, vmem, vmem, vmem],
        out_specs=hbm,
        scratch_shapes=[
            pltpu.VMEM((rows, side), BF16),
            whole, whole, whole, whole, whole,
            pltpu.VMEM((side, side), F32),
            pltpu.VMEM((side, 3 * NB), BF16),
            pltpu.VMEM((3 * NB, side), BF16),
            pltpu.VMEM((2 * NB, side), BF16),
            pltpu.VMEM((2 * NB, side), BF16),
            square, square,
            dma((4,)), dma((lanes,)), dma((lanes,)), dma((4,)),
            dma((steps, lanes)), dma((2, steps)), dma((steps,)),
        ],
        compiler_params=pltpu.CompilerParams(
            collective_id=0, has_side_effects=True, vmem_limit_bytes=VMEM_LIMIT
        ),
        cost_estimate=pl.CostEstimate(flops=14 * side**3, bytes_accessed=6 * side * side, transcendentals=0),
        name="refresh",
    )(row_counts, col_counts, grads[0], old_left[0], old_right[0])
    new_left, new_right = pl.pallas_call(
        hand_on,
        out_shape=(part, part),
        in_specs=[vmem],
        out_specs=(vmem, vmem),
        name="hand_on",
    )(both)
    return (new_left[None], new_right[None])


def solution(mesh):
    split = P("fsdp", "tensor", None)
    return jax.shard_map(
        body, mesh=mesh, in_specs=(split, P(), P(), split, split), out_specs=(split, split), check_vma=False
    )
```

```python
import functools

import jax
import jax.numpy as jnp
from jax import lax
from jax.experimental import pallas as pl
from jax.experimental.pallas import tpu as pltpu
from jax.sharding import PartitionSpec as P

MESH = pl.DeviceIdType.MESH
BF16 = jnp.bfloat16
F32 = jnp.float32
NB = 128
VMEM_LIMIT = 56 * 1024 * 1024


def workers(lanes):
    core = lax.rem(lax.axis_index("fsdp"), 2)
    left = core * (lanes // 4)
    return left, left + lanes // 2


def ring_barrier(lanes, me, meanwhile):
    barrier = pltpu.get_barrier_semaphore()
    for step in range(1, lanes):
        other = lax.rem(me + step, lanes)
        pl.semaphore_signal(barrier, inc=1, device_id={"tensor": other}, device_id_type=MESH)
    meanwhile()
    pl.semaphore_wait(barrier, lanes - 1)


def across(column):
    return jnp.broadcast_to(column, (8, NB))


def inverse_rcp(x):
    r = pl.reciprocal(x, approx=True)
    return r * (2.0 - x * r)


def group_update(body, inside, k0, rcp, upper, flat):
    cols = [across(body[:, k0 + q : k0 + q + 1]) for q in range(8)]
    body = jnp.where(inside, 0.0, body)
    for p in range(8):
        w = cols[p] * rcp[p]
        for q in range(p + 1, 8):
            cols[q] = cols[q] - w * upper[p][q]
        body = body - w * flat[p]
    return body


def diag_rounds(load, store):
    count = NB // 8
    sub = lax.broadcasted_iota(jnp.int32, (8, NB), 0)
    lane = lax.broadcasted_iota(jnp.int32, (8, NB), 1)
    rows = [load(i) for i in range(count)]
    for r in range(count):
        k0 = 8 * r
        inside = (lane >= k0) & (lane < k0 + 8)
        top = rows[r]
        cols = [across(top[:, k0 + q : k0 + q + 1]) for q in range(8)]
        u = [{q: across(cols[q][p : p + 1, :]) for q in range(p, 8)} for p in range(8)]
        top = jnp.where(lane - k0 == sub, 1.0, jnp.where(inside, 0.0, top))
        flat = [across(top[p : p + 1, :]) for p in range(8)]
        rcp = [None] * 8
        root = [None] * 8
        for p in range(0, 8, 2):
            n = p + 1
            det = u[p][p] * u[n][n] - u[p][n] * u[p][n]
            rcp[p] = inverse_rcp(u[p][p])
            rcp[n] = u[p][p] * inverse_rcp(det)
            root[p] = lax.rsqrt(u[p][p])
            root[n] = lax.rsqrt(det * rcp[p])
            low = {s: u[p][s] * rcp[p] for s in range(n, 8)}
            for t in range(n + 1, 8):
                u[n][t] = u[n][t] - low[n] * u[p][t]
            high = {s: u[n][s] * rcp[n] for s in range(n + 1, 8)}
            for s in range(n + 1, 8):
                for t in range(s, 8):
                    u[s][t] = u[s][t] - low[s] * u[p][t] - high[s] * u[n][t]
            flat[n] = flat[n] - low[n] * flat[p]
            for s in range(n + 1, 8):
                flat[s] = flat[s] - low[s] * flat[p] - high[s] * flat[n]
        for i in range(r + 1, min(r + 3, count)):
            rows[i] = group_update(rows[i], inside, k0, rcp, u, flat)
        scaled = jnp.zeros((8, NB), F32)
        for p in range(8):
            scaled = jnp.where(sub == p, flat[p] * root[p], scaled)
        store(r, jnp.where(lane <= sub + k0, scaled, 0.0))
        if r + 3 < count:
            high = scaled.astype(BF16).astype(F32)
            low = scaled - high
            zero = jnp.zeros((8, NB), F32)
            left = jnp.concatenate([high, low, high, zero], axis=0).astype(BF16)
            right = jnp.concatenate([high, high, low, zero], axis=0).astype(BF16)
            off = tn(left, right)
            for i in range(r + 3, count):
                rows[i] = jnp.where(inside, 0.0, rows[i]) - off[8 * i : 8 * i + 8, :]
        yield


def weave(rounds, chunks):
    chunks = list(chunks)
    total, rounds_total, given = len(chunks), NB // 8, 0
    for done, _ in enumerate(rounds, 1):
        upto = total * done // rounds_total
        for chunk in chunks[given:upto]:
            chunk()
        given = upto


def halves(x):
    high = x.astype(BF16)
    return high, (x - high.astype(F32)).astype(BF16)


def nt(a, b):
    return lax.dot_general(a, b, (((1,), (1,)), ((), ())), preferred_element_type=F32)


def nn(a, b):
    return jnp.dot(a, b, preferred_element_type=F32)


def tn(a, b):
    return lax.dot_general(a, b, (((0,), (0,)), ((), ())), preferred_element_type=F32)


def eliminate(step, phase, a_ref, m_ref, lcat, rcat, pair):
    side = a_ref.shape[0]
    start = pl.multiple_of(step * NB, NB)
    here = pl.ds(start, NB)
    tile = min(256, side)
    spans = [slice(t * tile, (t + 1) * tile) for t in range(side // tile)]

    def scale():
        mh, ml = halves(m_ref[...])
        scale_row(step, a_ref, m_ref, mh, ml, rcat, pair)

    def multiples(span):
        mh, ml = halves(m_ref[...])
        below = span.start + lax.broadcasted_iota(jnp.int32, (tile, NB), 0) >= start + NB
        column = a_ref[span, here]
        ch, cl = halves(jnp.where(below, column, 0.0))
        low = nt(jnp.concatenate([ch, cl, ch], axis=1), jnp.concatenate([mh, mh, ml], axis=1))
        lh, ll = halves(low)
        lcat[span, 0:NB] = lh
        lcat[span, NB : 2 * NB] = ll
        lcat[span, 2 * NB : 3 * NB] = lh
        a_ref[span, here] = jnp.where(below, 0.0, column)

    def trail(rows, cols):
        a_ref[rows, cols] = a_ref[rows, cols] - nn(lcat[rows, :], rcat[:, cols])

    pieces = [scale] + [functools.partial(multiples, span) for span in spans[phase:]]
    return pieces + [functools.partial(trail, rows, cols) for cols in spans for rows in spans[phase:]]


def scale_row(step, a_ref, m_ref, mh, ml, rcat, pair):
    side = a_ref.shape[0]
    start = pl.multiple_of(step * NB, NB)
    here = pl.ds(start, NB)
    bh, bl = halves(a_ref[here, :])
    fresh = nn(
        jnp.concatenate([mh, ml, mh], axis=1), jnp.concatenate([bh, bh, bl], axis=0)
    )
    a_ref[here, :] = fresh
    a_ref[here, here] = m_ref[...]
    fresh = a_ref[here, :]
    fh, fl = halves(fresh)
    rcat[0:NB, :] = fh
    rcat[NB : 2 * NB, :] = fh
    rcat[2 * NB : 3 * NB, :] = fl
    kept = lax.broadcasted_iota(jnp.int32, (NB, side), 1) < start + NB
    kh, kl = halves(jnp.where(kept, fresh, 0.0))
    pair[0:NB, :] = kh
    pair[NB : 2 * NB, :] = kl


def kernel(
    lanes, rc_ref, cc_ref, g_in, l_in, r_in, out,
    gm, gbuf, pbuf, s_ref, w_ref, x_ref, a_ref, lcat, rcat, pair, m_ref, d_ref,
    relay, ssem, gsem, psem, osem, xsend, xrecv, xown, hsem, fsem,
):
    me = lax.axis_index("tensor")
    block = lax.axis_index("fsdp")
    rows, side = g_in.shape
    steps = side // NB
    tile = min(256, side)
    left, right = workers(lanes)
    def rows_of(lane):
        return pl.ds(pl.multiple_of(lane * rows, rows), rows)

    mine = rows_of(me)

    def mask():
        rid = me * rows + lax.broadcasted_iota(jnp.int32, (rows, side), 0)
        cid = lax.broadcasted_iota(jnp.int32, (rows, side), 1)
        keep = (rid < rc_ref[block]) & (cid < cc_ref[block])
        gm[...] = jnp.where(keep, g_in[...].astype(F32), 0.0).astype(BF16)

    ring_barrier(lanes, me, mask)

    def remote(src, dst, k, sem, to):
        return pltpu.make_async_remote_copy(
            src_ref=src, dst_ref=dst.at[mine], send_sem=ssem.at[k], recv_sem=sem.at[me],
            device_id={"tensor": to}, device_id_type=MESH,
        )

    turn_of = 1 - 2 * lax.rem(block, 2)

    def via(to):
        return lax.rem(to + lanes // 2 + turn_of + lanes, lanes)

    def handed(kind, src, k):
        return pltpu.make_async_remote_copy(
            src_ref=src, dst_ref=relay.at[kind], send_sem=ssem.at[k], recv_sem=hsem.at[kind],
            device_id={"tensor": lax.rem(me + turn_of + lanes, lanes)}, device_id_type=MESH,
        )

    def hand_over(kind, dst, sem, to):
        source = lax.rem(to + lanes // 2, lanes)
        return pltpu.make_async_remote_copy(
            src_ref=relay.at[kind], dst_ref=dst.at[rows_of(source)], send_sem=fsem.at[kind], recv_sem=sem.at[source],
            device_id={"tensor": to}, device_id_type=MESH,
        )

    jobs = (
        (left, gm, gbuf, 0, gsem), (right, gm, gbuf, 1, gsem), (left, l_in, pbuf, 2, psem), (right, r_in, pbuf, 3, psem)
    )
    for to, src, dst, k, sem in jobs:
        opposite = me == lax.rem(to + lanes // 2, lanes)

        @pl.when(opposite)
        def _():
            handed(k // 2, src, k).start()

        @pl.when((me != to) & jnp.logical_not(opposite))
        def _():
            remote(src, dst, k, sem, to).start()

        @pl.when(me == to)
        def _():
            pltpu.make_async_copy(src, dst.at[mine], osem.at[k]).start()

    def finish_jobs(chosen):
        for to, src, dst, k, sem in chosen:
            @pl.when(me != to)
            def _():
                remote(src, dst, k, sem, to).wait_send()

            @pl.when(me == to)
            def _():
                pltpu.make_async_copy(src, dst.at[mine], osem.at[k]).wait()

    def arrived(src, dst, sem):
        for step in range(1, lanes):
            other = lax.rem(me + step, lanes)
            pltpu.make_async_remote_copy(
                src_ref=src, dst_ref=dst.at[rows_of(other)], send_sem=ssem.at[0], recv_sem=sem.at[other],
                device_id={"tensor": other}, device_id_type=MESH,
            ).wait_recv()

    def columns(step):
        return pl.ds(pl.multiple_of(step * NB, NB), NB)

    def give(which, step, turn):
        other = lax.rem(me + turn, lanes)
        return pltpu.make_async_remote_copy(
            src_ref=x_ref.at[rows_of(other), columns(step)], dst_ref=out.at[which, :, columns(step)],
            send_sem=xsend.at[step, turn], recv_sem=xrecv.at[which, step],
            device_id={"tensor": other}, device_id_type=MESH,
        )

    def own(which, step):
        return pltpu.make_async_copy(x_ref.at[mine, columns(step)], out.at[which, :, columns(step)], xown.at[step])

    def pair_product(t, depth):
        both = nt(w_ref[t * tile : (t + 1) * tile, :depth], pair[:, :depth])
        return both[:, :NB] + both[:, NB:]

    def product(step, phase):
        def piece(t):
            x_ref[t * tile : (t + 1) * tile, columns(step)] = pair_product(t, tile * (phase + 1)).astype(BF16)

        return [functools.partial(piece, t) for t in range(side // tile)]

    def unscaled_last():
        last = slice(side - NB, side)

        def rows():
            eye = lax.broadcasted_iota(jnp.int32, (NB, NB), 0) == lax.broadcasted_iota(jnp.int32, (NB, NB), 1)
            pair[0:NB, last] = jnp.where(eye, 1.0, 0.0).astype(BF16)
            pair[NB:, last] = jnp.zeros((NB, NB), BF16)
            if side > NB:
                high, low = halves(a_ref[last, : side - NB])
                pair[0:NB, : side - NB] = high
                pair[NB:, : side - NB] = low

        def piece(t):
            span = slice(t * tile, (t + 1) * tile)
            high, low = halves(pair_product(t, side))
            lcat[span, 0:NB] = high
            lcat[span, NB : 2 * NB] = low
            lcat[span, 2 * NB :] = high

        return [rows] + [functools.partial(piece, t) for t in range(side // tile)]

    def send(step):
        for turn in range(1, lanes):
            give(side_of, step, turn).start()
        own(side_of, step).start()

    def at(t):
        return pl.ds(pl.multiple_of(t * tile, tile), tile)

    def next_diag(step):
        later = columns(lax.rem(step + 1, steps))
        mh, ml = halves(m_ref[...])
        ch, cl = halves(a_ref[later, columns(step)])
        low = nt(jnp.concatenate([ch, cl, ch], axis=1), jnp.concatenate([mh, mh, ml], axis=1))
        lh, ll = halves(low)
        d_ref[...] = a_ref[later, later] - nt(
            jnp.concatenate([lh, ll, lh], axis=1), jnp.concatenate([lh, lh, ll], axis=1)
        )

    def begin(which):
        finish_jobs(jobs[which : which + 1])
        arrived(gm, gbuf, gsem)

        @pl.loop(0, side // tile)
        def _(t):
            if which == 0:
                stat = nt(gbuf[at(t), :], gbuf[...])
            else:
                stat = tn(gbuf[:, at(t)], gbuf[...])
            s_ref[at(t), :] = (stat * (1.0 / side)).astype(BF16)

        finish_jobs(jobs[2 + which : 3 + which])
        arrived(l_in, pbuf, psem)
        finish_jobs((jobs[1 - which], jobs[3 - which]))

    for which, worker in enumerate((left, right)):
        @pl.when(me == worker)
        def _():
            begin(which)

    for to in (left, right):
        @pl.when(me == via(to))
        def _():
            parts = ((0, gm, gbuf, gsem, 0), (1, l_in, pbuf, psem, 2))
            for kind, src, dst, sem, k in parts:
                handed(kind, src, k).wait_recv()
                hand_over(kind, dst, sem, to).start()
            for kind, src, dst, sem, k in parts:
                hand_over(kind, dst, sem, to).wait_send()

    working = (me == left) | (me == right)
    side_of = lax.div(lax.rem(me - left + lanes, lanes), lanes // 2)

    @pl.when(working)
    def _():
        @pl.loop(0, side // tile)
        def _(t):
            w_ref[at(t), :] = (nn(s_ref[at(t), :], pbuf[...]) + pbuf[at(t), :].astype(F32)).astype(BF16)

        d_ref[...] = tn(w_ref[:, 0:NB], w_ref[:, 0:NB])

        def invert(chunks):
            parts = []
            rounds = diag_rounds(lambda i: d_ref[8 * i : 8 * i + 8, :], lambda i, part: parts.append(part))
            weave(rounds, chunks)
            for i, part in enumerate(parts):
                m_ref[8 * i : 8 * i + 8, :] = part

        def gram(t):
            span = slice(t * tile, (t + 1) * tile)
            a_ref[span, :] = tn(w_ref[:, span], w_ref[...])

        invert([functools.partial(gram, t) for t in range(side // tile)])
        next_diag(0)

        each = tile // NB
        for phase in range(side // tile - 1 if side > tile else 0):
            @pl.loop(each * phase + 1, min(each * (phase + 1) + 1, steps - 1))
            def _(step):
                invert(eliminate(step - 1, phase, a_ref, m_ref, lcat, rcat, pair) + product(step - 1, phase))
                next_diag(step)
                send(step - 1)

        phase = side // tile - 1
        last = steps - 1
        invert(
            eliminate(last - 1, phase, a_ref, m_ref, lcat, rcat, pair) + product(last - 1, phase) + unscaled_last()
        )
        send(last - 1)
        mh, ml = halves(m_ref[...])
        for t in range(side // tile):
            span = slice(t * tile, (t + 1) * tile)
            x_ref[span, columns(last)] = nt(lcat[span, :], jnp.concatenate([mh, mh, ml], axis=1)).astype(BF16)
        send(last)

        @pl.loop(0, steps)
        def _(step):
            for turn in range(1, lanes):
                give(side_of, step, turn).wait_send()
            own(side_of, step).wait()

    @pl.when(jnp.logical_not(working))
    def _():
        finish_jobs(jobs)

    for which, worker in enumerate((left, right)):
        @pl.when(me != worker)
        def _():
            @pl.loop(0, steps)
            def _(step):
                give(which, step, 1).wait_recv()


def hand_on(both, first, second):
    first[...] = both[0]
    second[...] = both[1]


def body(grads, row_counts, col_counts, old_left, old_right):
    rows, side = grads.shape[1:]
    lanes = lax.axis_size("tensor")
    steps = side // NB
    vmem = pl.BlockSpec(memory_space=pltpu.VMEM)
    smem = pl.BlockSpec(memory_space=pltpu.SMEM)
    hbm = pl.BlockSpec(memory_space=pl.ANY)
    part = jax.ShapeDtypeStruct((rows, side), BF16)
    dma = pltpu.SemaphoreType.DMA
    whole = pltpu.VMEM((side, side), BF16)
    square = pltpu.VMEM((NB, NB), F32)
    both = pl.pallas_call(
        functools.partial(kernel, lanes),
        out_shape=jax.ShapeDtypeStruct((2, rows, side), BF16),
        in_specs=[smem, smem, vmem, vmem, vmem],
        out_specs=hbm,
        scratch_shapes=[
            pltpu.VMEM((rows, side), BF16),
            whole, whole, whole, whole, whole,
            pltpu.VMEM((side, side), F32),
            pltpu.VMEM((side, 3 * NB), BF16),
            pltpu.VMEM((3 * NB, side), BF16),
            pltpu.VMEM((2 * NB, side), BF16),
            square, square,
            pltpu.VMEM((2, rows, side), BF16),
            dma((4,)), dma((lanes,)), dma((lanes,)), dma((4,)),
            dma((steps, lanes)), dma((2, steps)), dma((steps,)), dma((2,)), dma((2,)),
        ],
        compiler_params=pltpu.CompilerParams(
            collective_id=0, has_side_effects=True, vmem_limit_bytes=VMEM_LIMIT
        ),
        cost_estimate=pl.CostEstimate(flops=14 * side**3, bytes_accessed=6 * side * side, transcendentals=0),
        name="refresh",
    )(row_counts, col_counts, grads[0], old_left[0], old_right[0])
    new_left, new_right = pl.pallas_call(
        hand_on,
        out_shape=(part, part),
        in_specs=[vmem],
        out_specs=(vmem, vmem),
        name="hand_on",
    )(both)
    return (new_left[None], new_right[None])


def solution(mesh):
    split = P("fsdp", "tensor", None)
    return jax.shard_map(
        body, mesh=mesh, in_specs=(split, P(), P(), split, split), out_specs=(split, split), check_vma=False
    )
```

```python
import functools

import jax
import jax.numpy as jnp
from jax import lax
from jax.experimental import pallas as pl
from jax.experimental.pallas import tpu as pltpu
from jax.sharding import PartitionSpec as P

MESH = pl.DeviceIdType.MESH
BF16 = jnp.bfloat16
F32 = jnp.float32
NB = 128
VMEM_LIMIT = 56 * 1024 * 1024


def workers(lanes):
    core = lax.rem(lax.axis_index("fsdp"), 2)
    left = core * (lanes // 4)
    return left, left + lanes // 2


def ring_barrier(lanes, me, meanwhile):
    barrier = pltpu.get_barrier_semaphore()
    for step in range(1, lanes):
        other = lax.rem(me + step, lanes)
        pl.semaphore_signal(barrier, inc=1, device_id={"tensor": other}, device_id_type=MESH)
    meanwhile()
    pl.semaphore_wait(barrier, lanes - 1)


def across(column):
    return jnp.broadcast_to(column, (8, NB))


def inverse_rcp(x):
    r = pl.reciprocal(x, approx=True)
    return r * (2.0 - x * r)


def group_update(body, inside, k0, rcp, upper, flat):
    cols = [across(body[:, k0 + q : k0 + q + 1]) for q in range(8)]
    body = jnp.where(inside, 0.0, body)
    for p in range(8):
        w = cols[p] * rcp[p]
        for q in range(p + 1, 8):
            cols[q] = cols[q] - w * upper[p][q]
        body = body - w * flat[p]
    return body


def diag_rounds(load, store):
    count = NB // 8
    sub = lax.broadcasted_iota(jnp.int32, (8, NB), 0)
    lane = lax.broadcasted_iota(jnp.int32, (8, NB), 1)
    rows = [load(i) for i in range(count)]
    for r in range(count):
        k0 = 8 * r
        inside = (lane >= k0) & (lane < k0 + 8)
        top = rows[r]
        cols = [across(top[:, k0 + q : k0 + q + 1]) for q in range(8)]
        u = [{q: across(cols[q][p : p + 1, :]) for q in range(p, 8)} for p in range(8)]
        top = jnp.where(lane - k0 == sub, 1.0, jnp.where(inside, 0.0, top))
        flat = [across(top[p : p + 1, :]) for p in range(8)]
        rcp = [None] * 8
        root = [None] * 8
        for p in range(0, 8, 2):
            n = p + 1
            det = u[p][p] * u[n][n] - u[p][n] * u[p][n]
            rcp[p] = inverse_rcp(u[p][p])
            rcp[n] = u[p][p] * inverse_rcp(det)
            root[p] = lax.rsqrt(u[p][p])
            root[n] = lax.rsqrt(det * rcp[p])
            low = {s: u[p][s] * rcp[p] for s in range(n, 8)}
            for t in range(n + 1, 8):
                u[n][t] = u[n][t] - low[n] * u[p][t]
            high = {s: u[n][s] * rcp[n] for s in range(n + 1, 8)}
            for s in range(n + 1, 8):
                for t in range(s, 8):
                    u[s][t] = u[s][t] - low[s] * u[p][t] - high[s] * u[n][t]
            flat[n] = flat[n] - low[n] * flat[p]
            for s in range(n + 1, 8):
                flat[s] = flat[s] - low[s] * flat[p] - high[s] * flat[n]
        for i in range(r + 1, min(r + 4, count)):
            rows[i] = group_update(rows[i], inside, k0, rcp, u, flat)
        scaled = jnp.zeros((8, NB), F32)
        for p in range(8):
            scaled = jnp.where(sub == p, flat[p] * root[p], scaled)
        store(r, jnp.where(lane <= sub + k0, scaled, 0.0))
        if r + 4 < count:
            high = scaled.astype(BF16).astype(F32)
            low = scaled - high
            zero = jnp.zeros((8, NB), F32)
            left = jnp.concatenate([high, low, high, zero], axis=0).astype(BF16)
            right = jnp.concatenate([high, high, low, zero], axis=0).astype(BF16)
            off = tn(left, right)
            for i in range(r + 4, count):
                rows[i] = jnp.where(inside, 0.0, rows[i]) - off[8 * i : 8 * i + 8, :]
        yield


def weave(rounds, chunks):
    chunks = list(chunks)
    total, rounds_total, given = len(chunks), NB // 8, 0
    for done, _ in enumerate(rounds, 1):
        upto = total * done // rounds_total
        for chunk in chunks[given:upto]:
            chunk()
        given = upto


def halves(x):
    high = x.astype(BF16)
    return high, (x - high.astype(F32)).astype(BF16)


def nt(a, b):
    return lax.dot_general(a, b, (((1,), (1,)), ((), ())), preferred_element_type=F32)


def nn(a, b):
    return jnp.dot(a, b, preferred_element_type=F32)


def tn(a, b):
    return lax.dot_general(a, b, (((0,), (0,)), ((), ())), preferred_element_type=F32)


def eliminate(step, phase, a_ref, m_ref, lcat, rcat, pair):
    side = a_ref.shape[0]
    start = pl.multiple_of(step * NB, NB)
    here = pl.ds(start, NB)
    tile = min(256, side)
    spans = [slice(t * tile, (t + 1) * tile) for t in range(side // tile)]

    def scale():
        mh, ml = halves(m_ref[...])
        scale_row(step, a_ref, m_ref, mh, ml, rcat, pair)

    def multiples(span):
        mh, ml = halves(m_ref[...])
        below = span.start + lax.broadcasted_iota(jnp.int32, (tile, NB), 0) >= start + NB
        column = a_ref[span, here]
        ch, cl = halves(jnp.where(below, column, 0.0))
        low = nt(jnp.concatenate([ch, cl, ch], axis=1), jnp.concatenate([mh, mh, ml], axis=1))
        lh, ll = halves(low)
        lcat[span, 0:NB] = lh
        lcat[span, NB : 2 * NB] = ll
        lcat[span, 2 * NB : 3 * NB] = lh
        a_ref[span, here] = jnp.where(below, 0.0, column)

    def trail(rows, cols):
        a_ref[rows, cols] = a_ref[rows, cols] - nn(lcat[rows, :], rcat[:, cols])

    pieces = [scale] + [functools.partial(multiples, span) for span in spans[phase:]]
    return pieces + [functools.partial(trail, rows, cols) for cols in spans for rows in spans[phase:]]


def scale_row(step, a_ref, m_ref, mh, ml, rcat, pair):
    side = a_ref.shape[0]
    start = pl.multiple_of(step * NB, NB)
    here = pl.ds(start, NB)
    bh, bl = halves(a_ref[here, :])
    fresh = nn(
        jnp.concatenate([mh, ml, mh], axis=1), jnp.concatenate([bh, bh, bl], axis=0)
    )
    a_ref[here, :] = fresh
    a_ref[here, here] = m_ref[...]
    fresh = a_ref[here, :]
    fh, fl = halves(fresh)
    rcat[0:NB, :] = fh
    rcat[NB : 2 * NB, :] = fh
    rcat[2 * NB : 3 * NB, :] = fl
    kept = lax.broadcasted_iota(jnp.int32, (NB, side), 1) < start + NB
    kh, kl = halves(jnp.where(kept, fresh, 0.0))
    pair[0:NB, :] = kh
    pair[NB : 2 * NB, :] = kl


def kernel(
    lanes, rc_ref, cc_ref, g_in, l_in, r_in, out,
    gm, gbuf, pbuf, s_ref, w_ref, x_ref, a_ref, lcat, rcat, pair, m_ref, d_ref,
    relay, ssem, gsem, psem, osem, xsend, xrecv, xown, hsem, fsem,
):
    me = lax.axis_index("tensor")
    block = lax.axis_index("fsdp")
    rows, side = g_in.shape
    steps = side // NB
    tile = min(256, side)
    left, right = workers(lanes)
    def rows_of(lane):
        return pl.ds(pl.multiple_of(lane * rows, rows), rows)

    mine = rows_of(me)

    def mask():
        rid = me * rows + lax.broadcasted_iota(jnp.int32, (rows, side), 0)
        cid = lax.broadcasted_iota(jnp.int32, (rows, side), 1)
        keep = (rid < rc_ref[block]) & (cid < cc_ref[block])
        gm[...] = jnp.where(keep, g_in[...].astype(F32), 0.0).astype(BF16)

    ring_barrier(lanes, me, mask)

    def remote(src, dst, k, sem, to):
        return pltpu.make_async_remote_copy(
            src_ref=src, dst_ref=dst.at[mine], send_sem=ssem.at[k], recv_sem=sem.at[me],
            device_id={"tensor": to}, device_id_type=MESH,
        )

    turn_of = 1 - 2 * lax.rem(block, 2)

    def via(to):
        return lax.rem(to + lanes // 2 + turn_of + lanes, lanes)

    def handed(kind, src, k):
        return pltpu.make_async_remote_copy(
            src_ref=src, dst_ref=relay.at[kind], send_sem=ssem.at[k], recv_sem=hsem.at[kind],
            device_id={"tensor": lax.rem(me + turn_of + lanes, lanes)}, device_id_type=MESH,
        )

    def hand_over(kind, dst, sem, to):
        source = lax.rem(to + lanes // 2, lanes)
        return pltpu.make_async_remote_copy(
            src_ref=relay.at[kind], dst_ref=dst.at[rows_of(source)], send_sem=fsem.at[kind], recv_sem=sem.at[source],
            device_id={"tensor": to}, device_id_type=MESH,
        )

    jobs = (
        (left, gm, gbuf, 0, gsem), (right, gm, gbuf, 1, gsem), (left, l_in, pbuf, 2, psem), (right, r_in, pbuf, 3, psem)
    )
    for to, src, dst, k, sem in jobs:
        opposite = me == lax.rem(to + lanes // 2, lanes)

        @pl.when(opposite)
        def _():
            handed(k // 2, src, k).start()

        @pl.when((me != to) & jnp.logical_not(opposite))
        def _():
            remote(src, dst, k, sem, to).start()

        @pl.when(me == to)
        def _():
            pltpu.make_async_copy(src, dst.at[mine], osem.at[k]).start()

    def finish_jobs(chosen):
        for to, src, dst, k, sem in chosen:
            @pl.when(me != to)
            def _():
                remote(src, dst, k, sem, to).wait_send()

            @pl.when(me == to)
            def _():
                pltpu.make_async_copy(src, dst.at[mine], osem.at[k]).wait()

    def arrived(src, dst, sem):
        for step in range(1, lanes):
            other = lax.rem(me + step, lanes)
            pltpu.make_async_remote_copy(
                src_ref=src, dst_ref=dst.at[rows_of(other)], send_sem=ssem.at[0], recv_sem=sem.at[other],
                device_id={"tensor": other}, device_id_type=MESH,
            ).wait_recv()

    def columns(step):
        return pl.ds(pl.multiple_of(step * NB, NB), NB)

    def give(which, step, turn):
        other = lax.rem(me + turn, lanes)
        return pltpu.make_async_remote_copy(
            src_ref=x_ref.at[rows_of(other), columns(step)], dst_ref=out.at[which, :, columns(step)],
            send_sem=xsend.at[step, turn], recv_sem=xrecv.at[which, step],
            device_id={"tensor": other}, device_id_type=MESH,
        )

    def own(which, step):
        return pltpu.make_async_copy(x_ref.at[mine, columns(step)], out.at[which, :, columns(step)], xown.at[step])

    def pair_product(t, depth):
        both = nt(w_ref[t * tile : (t + 1) * tile, :depth], pair[:, :depth])
        return both[:, :NB] + both[:, NB:]

    def product(step, phase):
        def piece(t):
            x_ref[t * tile : (t + 1) * tile, columns(step)] = pair_product(t, tile * (phase + 1)).astype(BF16)

        return [functools.partial(piece, t) for t in range(side // tile)]

    def unscaled_last():
        last = slice(side - NB, side)

        def rows():
            eye = lax.broadcasted_iota(jnp.int32, (NB, NB), 0) == lax.broadcasted_iota(jnp.int32, (NB, NB), 1)
            pair[0:NB, last] = jnp.where(eye, 1.0, 0.0).astype(BF16)
            pair[NB:, last] = jnp.zeros((NB, NB), BF16)
            if side > NB:
                high, low = halves(a_ref[last, : side - NB])
                pair[0:NB, : side - NB] = high
                pair[NB:, : side - NB] = low

        def piece(t):
            span = slice(t * tile, (t + 1) * tile)
            high, low = halves(pair_product(t, side))
            lcat[span, 0:NB] = high
            lcat[span, NB : 2 * NB] = low
            lcat[span, 2 * NB :] = high

        return [rows] + [functools.partial(piece, t) for t in range(side // tile)]

    def send(step):
        for turn in range(1, lanes):
            give(side_of, step, turn).start()
        own(side_of, step).start()

    def at(t):
        return pl.ds(pl.multiple_of(t * tile, tile), tile)

    def next_diag(step):
        later = columns(lax.rem(step + 1, steps))
        mh, ml = halves(m_ref[...])
        ch, cl = halves(a_ref[later, columns(step)])
        low = nt(jnp.concatenate([ch, cl, ch], axis=1), jnp.concatenate([mh, mh, ml], axis=1))
        lh, ll = halves(low)
        d_ref[...] = a_ref[later, later] - nt(
            jnp.concatenate([lh, ll, lh], axis=1), jnp.concatenate([lh, lh, ll], axis=1)
        )

    def begin(which):
        finish_jobs(jobs[which : which + 1])
        arrived(gm, gbuf, gsem)

        @pl.loop(0, side // tile)
        def _(t):
            if which == 0:
                stat = nt(gbuf[at(t), :], gbuf[...])
            else:
                stat = tn(gbuf[:, at(t)], gbuf[...])
            s_ref[at(t), :] = (stat * (1.0 / side)).astype(BF16)

        finish_jobs(jobs[2 + which : 3 + which])
        arrived(l_in, pbuf, psem)
        finish_jobs((jobs[1 - which], jobs[3 - which]))

    for which, worker in enumerate((left, right)):
        @pl.when(me == worker)
        def _():
            begin(which)

    for to in (left, right):
        @pl.when(me == via(to))
        def _():
            parts = ((0, gm, gbuf, gsem, 0), (1, l_in, pbuf, psem, 2))
            for kind, src, dst, sem, k in parts:
                handed(kind, src, k).wait_recv()
                hand_over(kind, dst, sem, to).start()
            for kind, src, dst, sem, k in parts:
                hand_over(kind, dst, sem, to).wait_send()

    working = (me == left) | (me == right)
    side_of = lax.div(lax.rem(me - left + lanes, lanes), lanes // 2)

    @pl.when(working)
    def _():
        @pl.loop(0, side // tile)
        def _(t):
            w_ref[at(t), :] = (nn(s_ref[at(t), :], pbuf[...]) + pbuf[at(t), :].astype(F32)).astype(BF16)

        d_ref[...] = tn(w_ref[:, 0:NB], w_ref[:, 0:NB])

        def invert(chunks):
            parts = []
            rounds = diag_rounds(lambda i: d_ref[8 * i : 8 * i + 8, :], lambda i, part: parts.append(part))
            weave(rounds, chunks)
            for i, part in enumerate(parts):
                m_ref[8 * i : 8 * i + 8, :] = part

        def gram(t):
            span = slice(t * tile, (t + 1) * tile)
            a_ref[span, :] = tn(w_ref[:, span], w_ref[...])

        invert([functools.partial(gram, t) for t in range(side // tile)])
        next_diag(0)

        each = tile // NB
        for phase in range(side // tile - 1 if side > tile else 0):
            @pl.loop(each * phase + 1, min(each * (phase + 1) + 1, steps - 1))
            def _(step):
                invert(eliminate(step - 1, phase, a_ref, m_ref, lcat, rcat, pair) + product(step - 1, phase))
                next_diag(step)
                send(step - 1)

        phase = side // tile - 1
        last = steps - 1
        invert(
            eliminate(last - 1, phase, a_ref, m_ref, lcat, rcat, pair) + product(last - 1, phase) + unscaled_last()
        )
        send(last - 1)
        mh, ml = halves(m_ref[...])
        for t in range(side // tile):
            span = slice(t * tile, (t + 1) * tile)
            x_ref[span, columns(last)] = nt(lcat[span, :], jnp.concatenate([mh, mh, ml], axis=1)).astype(BF16)
        send(last)

        @pl.loop(0, steps)
        def _(step):
            for turn in range(1, lanes):
                give(side_of, step, turn).wait_send()
            own(side_of, step).wait()

    @pl.when(jnp.logical_not(working))
    def _():
        finish_jobs(jobs)

    for which, worker in enumerate((left, right)):
        @pl.when(me != worker)
        def _():
            @pl.loop(0, steps)
            def _(step):
                give(which, step, 1).wait_recv()


def hand_on(both, first, second):
    first[...] = both[0]
    second[...] = both[1]


def body(grads, row_counts, col_counts, old_left, old_right):
    rows, side = grads.shape[1:]
    lanes = lax.axis_size("tensor")
    steps = side // NB
    vmem = pl.BlockSpec(memory_space=pltpu.VMEM)
    smem = pl.BlockSpec(memory_space=pltpu.SMEM)
    hbm = pl.BlockSpec(memory_space=pl.ANY)
    part = jax.ShapeDtypeStruct((rows, side), BF16)
    dma = pltpu.SemaphoreType.DMA
    whole = pltpu.VMEM((side, side), BF16)
    square = pltpu.VMEM((NB, NB), F32)
    both = pl.pallas_call(
        functools.partial(kernel, lanes),
        out_shape=jax.ShapeDtypeStruct((2, rows, side), BF16),
        in_specs=[smem, smem, vmem, vmem, vmem],
        out_specs=hbm,
        scratch_shapes=[
            pltpu.VMEM((rows, side), BF16),
            whole, whole, whole, whole, whole,
            pltpu.VMEM((side, side), F32),
            pltpu.VMEM((side, 3 * NB), BF16),
            pltpu.VMEM((3 * NB, side), BF16),
            pltpu.VMEM((2 * NB, side), BF16),
            square, square,
            pltpu.VMEM((2, rows, side), BF16),
            dma((4,)), dma((lanes,)), dma((lanes,)), dma((4,)),
            dma((steps, lanes)), dma((2, steps)), dma((steps,)), dma((2,)), dma((2,)),
        ],
        compiler_params=pltpu.CompilerParams(
            collective_id=0, has_side_effects=True, vmem_limit_bytes=VMEM_LIMIT
        ),
        cost_estimate=pl.CostEstimate(flops=14 * side**3, bytes_accessed=6 * side * side, transcendentals=0),
        name="refresh",
    )(row_counts, col_counts, grads[0], old_left[0], old_right[0])
    new_left, new_right = pl.pallas_call(
        hand_on,
        out_shape=(part, part),
        in_specs=[vmem],
        out_specs=(vmem, vmem),
        name="hand_on",
    )(both)
    return (new_left[None], new_right[None])


def solution(mesh):
    split = P("fsdp", "tensor", None)
    return jax.shard_map(
        body, mesh=mesh, in_specs=(split, P(), P(), split, split), out_specs=(split, split), check_vma=False
    )
```
